32 devices in a mesh: row: 8 (over z, x), feat: 4 (over y, core).
Axes of the slice: x: 2, y: 2, z: 4, core: 2. Of those that a mesh axis runs over, the one named last changes fastest.
Arguments:
- bin_codes: int32 [256, 65536], P(None, 'row'), may hold values from 0 to 31
- gradients: bfloat16 [65536], P('row'), may hold values from -6 to 6
- hessians: bfloat16 [65536], P('row'), may hold values from 0.019897461 to 0.25
- pair_list: int32 [64, 2], replicated, may hold values from 0 to 255, as said below
- owners: int32 [64], replicated, may hold values from 0 to 3, as said below
Outputs:
- cut_table: float32 [128, 1024], P('feat', 'row')
- best_gain: float32 [64], replicated
The draws below stay inside these ranges and needn't reach their ends.
Inputs may be any that keep to these rules, and one draw needn't show every extreme that they name: `pair_list`: each row holds two different features, the first smaller. `owners`: one index owns exactly 32 pairs in every draw, the others at most that many.
All inputs are finite; a program needn't handle non-finite values.
Results may differ from the reference program's by a relative error of at most 0.0003.
Values sent between devices are 32-bit elements; how exact they have to be, the bound alone decides.
No kernel may reach another device: no remote copies, remote signals or barrier semaphores. Data moves between devices by JAX's collectives and lax.ppermute only.
A program may use at most 64 MiB of HBM per device.

```python
import math
import jax
import jax.numpy as jnp
from jax import lax

F = 256
BINS = 32
P_SIZE = 64
ROWS = 65536
SLOTS = 32
N_FEAT = 4


def draw_pair_list(key, part):
    first_key = jax.random.fold_in(key, 11)
    step_key = jax.random.fold_in(key, 12)
    first = jax.random.randint(first_key, (P_SIZE,), 0, F, dtype=jnp.int32)
    offset = jax.random.randint(step_key, (P_SIZE,), 1, F, dtype=jnp.int32)
    second = (first + offset) % F
    return jnp.stack([jnp.minimum(first, second), jnp.maximum(first, second)], axis=1).astype(jnp.int32)


def draw_owners(key, part):
    order_key = jax.random.fold_in(key, 21)
    heavy_key = jax.random.fold_in(key, 22)
    order = jax.random.permutation(order_key, P_SIZE).astype(jnp.int32)
    heavy = jax.random.randint(heavy_key, (), 0, N_FEAT, dtype=jnp.int32)
    places = jnp.arange(P_SIZE, dtype=jnp.int32)
    others = (heavy + 1 + (places - SLOTS) % (N_FEAT - 1)) % N_FEAT
    assigned = jnp.where(places < SLOTS, heavy, others).astype(jnp.int32)
    inverse = jnp.argsort(order, stable=True)
    return assigned[inverse].astype(jnp.int32)


def plant(values, rng, low, high):
    shape = values.shape
    index_at = [jax.random.randint(jax.random.fold_in(rng, axis), (), 0, shape[axis]) for axis in range(len(shape))]
    values = values.at[tuple(index_at)].set(low)
    longest = shape.index(max(shape))
    index_at[longest] = (index_at[longest] + 1) % shape[longest]
    return values.at[tuple(index_at)].set(high)


def steps_of(stream_key, dims, shards, low, largest):
    def one(dim, shards_of):
        draws = jax.random.uniform(jax.random.fold_in(jax.random.fold_in(stream_key, 6), dim), (shards_of,), jnp.float32, low / len(shards), largest / len(shards))
        return jnp.repeat(jnp.exp(draws), dims[dim] // shards_of).reshape((-1,) + (1,) * (len(dims) - dim - 1))

    level = one(*shards[0])
    for cut in shards[1:]:
        level = level * one(*cut)
    return level


def centred(key, shape, spread, reach, shards=(), kind=jnp.bfloat16):
    array = jax.random.normal(key, shape, jnp.float32) * spread
    if len(shards) > 0:
        array = steps_of(key, shape, shards, -0.22, 0.18) * array
    return jnp.clip(array, min=-reach, max=reach).astype(kind)


def setup_inputs(seed: int = 0) -> dict:
    streams_of = jax.random.split(jax.random.key(seed), 6)
    return {
        "bin_codes": plant(jax.random.randint(streams_of[0], (F, ROWS), 0, BINS), jax.random.fold_in(streams_of[0], 1), 0, BINS - 1).astype(jnp.int32),
        "gradients": centred(streams_of[1], (ROWS,), 1.0, 6.0, ((0, 8),)),
        "hessians": jnp.clip(jnp.exp(math.log(0.25) - 2.5308688 * jax.random.uniform(streams_of[2], (ROWS,), jnp.float32) ** steps_of(streams_of[2], (ROWS,), ((0, 8),), -0.2, 0.2)), 0.019897461, 0.25).astype(jnp.bfloat16),
        "pair_list": draw_pair_list(jax.random.fold_in(streams_of[5], 71), 0),
        "owners": draw_owners(jax.random.fold_in(streams_of[5], 71), 0),
    }


LAMBDA_REG = 1.0


def slot_rank(owners):
    pair_ids = jnp.arange(owners.shape[0], dtype=jnp.int32)
    same_owner = owners[:, None] == owners[None, :]
    earlier = pair_ids[None, :] < pair_ids[:, None]
    return jnp.sum((same_owner & earlier).astype(jnp.int32), axis=1)


def cumulate(histogram):
    bin_count = histogram.shape[-2]
    running = jnp.cumsum(histogram, axis=-2)
    shaped = running.reshape(running.shape[:-1] + (2, bin_count))
    shaped = jnp.cumsum(shaped, axis=-1)
    return shaped.reshape(running.shape)


def cut_gains(cut_rows, margin_row):
    bin_count = margin_row.shape[-1] // 2
    grad_cum = cut_rows[..., :bin_count]
    hess_cum = cut_rows[..., bin_count:]
    grad_end = grad_cum[..., -1:]
    hess_end = hess_cum[..., -1:]
    grad_col = margin_row[..., None, :bin_count]
    hess_col = margin_row[..., None, bin_count:]
    grad_all = margin_row[..., None, bin_count - 1:bin_count]
    hess_all = margin_row[..., None, 2 * bin_count - 1:]
    quad_grad = (grad_cum, grad_end - grad_cum, grad_col - grad_cum, grad_all - grad_end - grad_col + grad_cum)
    quad_hess = (hess_cum, hess_end - hess_cum, hess_col - hess_cum, hess_all - hess_end - hess_col + hess_cum)
    result = -(grad_all * grad_all) / (hess_all + LAMBDA_REG)
    for grad_part, hess_part in zip(quad_grad, quad_hess):
        result = result + grad_part * grad_part / (hess_part + LAMBDA_REG)
    return result


def pair_histogram(bin_codes, gradients, hessians, pair_row):
    levels = jnp.arange(BINS, dtype=jnp.int32)
    first_col = lax.dynamic_index_in_dim(bin_codes, pair_row[0], 0, keepdims=False)
    second_col = lax.dynamic_index_in_dim(bin_codes, pair_row[1], 0, keepdims=False)
    hot_first = (first_col[:, None] == levels[None, :]).astype(jnp.float32)
    hot_second = (second_col[:, None] == levels[None, :]).astype(jnp.float32)
    weighted = jnp.concatenate([hot_second * gradients.astype(jnp.float32)[:, None], hot_second * hessians.astype(jnp.float32)[:, None]], axis=1)
    return jnp.dot(hot_first.T, weighted, precision=lax.Precision.HIGHEST, preferred_element_type=jnp.float32)


def reference(bin_codes, gradients, hessians, pair_list, owners):
    histogram = lax.map(lambda pair_row: pair_histogram(bin_codes, gradients, hessians, pair_row), pair_list)
    running = cumulate(histogram)
    cut_gain = cut_gains(running, running[:, -1, :]).reshape(P_SIZE, BINS * BINS)
    best_gain = jnp.max(cut_gain, axis=1)
    rank = slot_rank(owners)
    table_ids = jnp.arange(N_FEAT * SLOTS, dtype=jnp.int32)
    owner_of = table_ids // SLOTS
    place_of = table_ids % SLOTS
    matched = (owners[None, :] == owner_of[:, None]) & (rank[None, :] == place_of[:, None])
    pair_ids = jnp.arange(P_SIZE, dtype=jnp.int32)
    chosen = jnp.sum(jnp.where(matched, pair_ids[None, :], 0), axis=1).astype(jnp.int32)
    has_pair = jnp.any(matched, axis=1)
    cut_table = jnp.where(has_pair[:, None], cut_gain[chosen], jnp.float32(0.0))
    return cut_table, best_gain
```

```python
import functools

import jax
import jax.numpy as jnp
from jax import lax
from jax.experimental import pallas as pl
from jax.experimental.pallas import tpu as pltpu
from jax.sharding import PartitionSpec as P

BINS = 32
LAMBDA_REG = 1.0
LANES = 128
GROUP = 4
PER_MESSAGE = 2
PARTS = 4
CHUNK = 2048


def cut_sums_kernel(feat_slots, pairs_hbm, codes_hbm, grad_hbm, hess_hbm, out_ref, pairs, codes, grad, hess, grad_wide, hess_wide, sums, code_sems, small_sems):
    groups = feat_slots // GROUP
    first_pair = lax.axis_index("feat") * feat_slots
    row_count = codes.shape[1]
    pairs_copy = pltpu.make_async_copy(pairs_hbm, pairs, small_sems.at[0])
    grad_copy = pltpu.make_async_copy(grad_hbm, grad, small_sems.at[1])
    hess_copy = pltpu.make_async_copy(hess_hbm, hess, small_sems.at[2])
    pairs_copy.start()
    grad_copy.start()
    hess_copy.start()
    pairs_copy.wait()
    code_copies = []
    for slot in range(feat_slots):
        for side in range(2):
            line = 2 * slot + side
            copy = pltpu.make_async_copy(
                codes_hbm.at[pl.ds(pairs[side, first_pair + slot], 1)], codes.at[pl.ds(line, 1)], code_sems.at[line]
            )
            copy.start()
            code_copies.append(copy)
    sums[...] = jnp.zeros_like(sums)
    half = BINS // 2
    levels = lax.broadcasted_iota(jnp.int32, (half, 1), 0).astype(jnp.float32)
    level_parts = (levels.astype(jnp.bfloat16), (levels + half).astype(jnp.bfloat16))
    grad_copy.wait()
    hess_copy.wait()
    for narrow, wide in ((grad, grad_wide), (hess, hess_wide)):
        values = narrow[...].astype(jnp.float32)
        for tile in range(row_count // LANES):
            line = jnp.broadcast_to(values[tile : tile + 1], (half, LANES))
            wide[:, tile * LANES : (tile + 1) * LANES] = line.astype(jnp.bfloat16)
    zero = jnp.zeros((half, CHUNK), jnp.bfloat16)
    one = jnp.ones((half, CHUNK), jnp.bfloat16)
    for copy in code_copies:
        copy.wait()

    def spread(line, span):
        values = codes[pl.ds(line, 1), span].astype(jnp.float32)
        return jnp.broadcast_to(values, (half, CHUNK)).astype(jnp.bfloat16)

    def step(index, carry):
        span = pl.ds(pl.multiple_of(index * CHUNK, CHUNK), CHUNK)
        grad_part = grad_wide[:, span]
        hess_part = hess_wide[:, span]
        for group in range(groups):
            grad_rows, hess_rows, second_rows = [], [], []
            for pair in range(GROUP):
                line = 2 * (GROUP * group + pair)
                first = spread(line, span)
                second = spread(line + 1, span)
                for level in level_parts:
                    below = first <= level
                    grad_rows.append(jnp.where(below, grad_part, zero))
                    hess_rows.append(jnp.where(below, hess_part, zero))
                    second_rows.append(jnp.where(second <= level, one, zero))
            weighted = jnp.concatenate(grad_rows + hess_rows, axis=0)
            hot = jnp.concatenate(second_rows, axis=0)
            sums[group] += lax.dot_general(
                weighted, hot, (((1,), (1,)), ((), ())), preferred_element_type=jnp.float32
            )
        return carry

    lax.fori_loop(0, row_count // CHUNK, step, 0)
    lane = lax.broadcasted_iota(jnp.int32, (BINS, LANES), 1)
    low = lane < LANES // 2

    def own_blocks(group, start):
        block = sums[group, start : start + BINS]
        for pair in range(1, GROUP):
            at = start + pair * BINS
            block = jnp.where(lane >= pair * BINS, sums[group, at : at + BINS], block)
        return block

    for group in range(groups):
        grad_cum = own_blocks(group, 0)
        hess_cum = own_blocks(group, GROUP * BINS)
        out_ref[2 * group] = jnp.where(low, grad_cum, pltpu.roll(hess_cum, LANES // 2, 1))
        out_ref[2 * group + 1] = jnp.where(low, pltpu.roll(grad_cum, LANES // 2, 1), hess_cum)
    for message in range(2 * groups, out_ref.shape[0]):
        out_ref[message] = jnp.zeros((BINS, LANES), jnp.float32)


def cut_sums(bin_codes, gradients, hessians, pair_list, feat_slots, messages):
    row_count = bin_codes.shape[1]
    groups = feat_slots // GROUP
    tiles = row_count // LANES
    anywhere = pl.BlockSpec(memory_space=pl.ANY)
    return pl.pallas_call(
        functools.partial(cut_sums_kernel, feat_slots),
        out_shape=jax.ShapeDtypeStruct((messages, BINS, LANES), jnp.float32),
        in_specs=[anywhere] * 4,
        out_specs=pl.BlockSpec(memory_space=pltpu.VMEM),
        scratch_shapes=[
            pltpu.SMEM((2, pair_list.shape[0]), jnp.int32),
            pltpu.VMEM((2 * feat_slots, row_count), jnp.int32),
            pltpu.VMEM((tiles, LANES), jnp.bfloat16),
            pltpu.VMEM((tiles, LANES), jnp.bfloat16),
            pltpu.VMEM((BINS // 2, row_count), jnp.bfloat16),
            pltpu.VMEM((BINS // 2, row_count), jnp.bfloat16),
            pltpu.VMEM((groups, 2 * GROUP * BINS, GROUP * BINS), jnp.float32),
            pltpu.SemaphoreType.DMA((2 * feat_slots,)),
            pltpu.SemaphoreType.DMA((3,)),
        ],
        compiler_params=pltpu.CompilerParams(vmem_limit_bytes=56 * 2**20),
    )(pair_list.T, bin_codes, gradients.reshape(tiles, LANES), hessians.reshape(tiles, LANES))


def gains_kernel(feat_slots, parts_ref, out_ref, gains):
    row_count, feat_count = out_ref.shape[0], out_ref.shape[1]
    share = BINS // row_count
    total = parts_ref[0]
    for part in range(1, parts_ref.shape[0]):
        total = total + parts_ref[part]
    lane = lax.broadcasted_iota(jnp.int32, (BINS, LANES), 1)
    first_half = lane < BINS

    def ends(cum):
        return jnp.where(first_half, cum[:, BINS - 1 : BINS], cum[:, 2 * BINS - 1 : 2 * BINS])

    grad_cum = total
    hess_cum = pltpu.roll(total, LANES // 2, 1)
    grad_end, hess_end = ends(grad_cum), ends(hess_cum)
    grad_col, hess_col = grad_cum[BINS - 1 :], hess_cum[BINS - 1 :]
    grad_all, hess_all = grad_end[BINS - 1 :], hess_end[BINS - 1 :]
    result = -(grad_all * grad_all) / (hess_all + LAMBDA_REG)
    for grad_part, hess_part in (
        (grad_cum, hess_cum),
        (grad_end - grad_cum, hess_end - hess_cum),
        (grad_col - grad_cum, hess_col - hess_cum),
        (grad_all - grad_end - grad_col + grad_cum, hess_all - hess_end - hess_col + hess_cum),
    ):
        result = result + grad_part * grad_part / (hess_part + LAMBDA_REG)
    gains[...] = result
    peak = jnp.max(result, axis=0, keepdims=True)
    line = lax.broadcasted_iota(jnp.int32, (1, LANES), 1)
    row_index = lax.axis_index("row")
    first_pair = lax.axis_index("feat") * feat_slots + PER_MESSAGE * row_index
    held = row_index < feat_slots // PER_MESSAGE
    best = jnp.zeros((1, LANES), jnp.float32)
    for pair in range(PER_MESSAGE):
        inside = (line >= pair * BINS) & (line < (pair + 1) * BINS)
        top = jnp.max(jnp.where(inside, peak, -jnp.inf), axis=1, keepdims=True)
        best = jnp.where((line == first_pair + pair) & held, top, best)
    wide = lax.broadcasted_iota(jnp.int32, (row_count, LANES), 1)
    cuts = []
    for pair in range(PER_MESSAGE):
        laid = jnp.zeros((row_count, LANES), jnp.float32)
        for step in range(share):
            lines = gains[pl.ds(step, row_count, stride=share), :] if share > 1 else gains[...]
            moved = (step - pair) * BINS % LANES
            if moved:
                lines = pltpu.roll(lines, moved, 1)
            laid = jnp.where((wide >= step * BINS) & (wide < (step + 1) * BINS), lines, laid)
        cuts.append(laid)
    spot = lax.broadcasted_iota(jnp.int32, (PARTS, LANES), 0)
    for row in range(row_count):
        message = jnp.where(spot == 0, cuts[0][row : row + 1], jnp.where(spot == 1, cuts[1][row : row + 1], best))
        for feat in range(feat_count):
            out_ref[row, feat] = message


def table_kernel(feat_slots, feat_count, owners_ref, parts_ref, table_ref, best_ref, table):
    feat_index = lax.axis_index("feat")
    home_slots, width = table_ref.shape
    table[...] = jnp.zeros_like(table)
    taken = jnp.int32(0)
    for pair in range(owners_ref.shape[0]):
        place = pair % feat_slots
        source = place // PER_MESSAGE * feat_count + pair // feat_slots
        mine = owners_ref[pair] == feat_index
        slot = jnp.where(mine, jnp.minimum(taken, home_slots), home_slots)
        table[pl.ds(slot, 1), :] = parts_ref[source, place % PER_MESSAGE : place % PER_MESSAGE + 1, :]
        taken = taken + mine.astype(jnp.int32)
    table_ref[...] = table[:home_slots, :width]
    best = jnp.sum(parts_ref[:, PER_MESSAGE, :], axis=0, keepdims=True)
    best_ref[...] = best[:, : best_ref.shape[1]]


def shards(bin_codes, gradients, hessians, pair_list, owners):
    feat_count = lax.axis_size("feat")
    row_count = lax.axis_size("row")
    pair_count = pair_list.shape[0]
    feat_slots = pair_count // feat_count
    home_slots = 2 * pair_count // feat_count
    width = BINS // row_count * BINS
    in_vmem = pl.BlockSpec(memory_space=pltpu.VMEM)
    partial = cut_sums(bin_codes, gradients, hessians, pair_list, feat_slots, row_count)
    parts = lax.all_to_all(partial, "row", split_axis=0, concat_axis=0, tiled=True)
    outgoing = pl.pallas_call(
        functools.partial(gains_kernel, feat_slots),
        out_shape=jax.ShapeDtypeStruct((row_count, feat_count, PARTS, LANES), jnp.float32),
        in_specs=[in_vmem],
        out_specs=in_vmem,
        scratch_shapes=[pltpu.VMEM((BINS, LANES), jnp.float32)],
    )(parts)
    outgoing = outgoing.reshape(row_count * feat_count, PARTS, LANES)
    incoming = lax.all_to_all(outgoing, ("row", "feat"), split_axis=0, concat_axis=0, tiled=True)
    cut_table, best = pl.pallas_call(
        functools.partial(table_kernel, feat_slots, feat_count),
        out_shape=(
            jax.ShapeDtypeStruct((home_slots, width), jnp.float32),
            jax.ShapeDtypeStruct((1, pair_count), jnp.float32),
        ),
        in_specs=[pl.BlockSpec(memory_space=pltpu.SMEM), in_vmem],
        out_specs=(in_vmem, in_vmem),
        scratch_shapes=[pltpu.VMEM((home_slots + 8, LANES), jnp.float32)],
    )(owners, incoming)
    return (cut_table, best.reshape(pair_count))


def solution(mesh):
    in_specs = (P(None, "row"), P("row"), P("row"), P(), P())
    out_specs = (P("feat", "row"), P())
    return jax.shard_map(shards, mesh=mesh, in_specs=in_specs, out_specs=out_specs, check_vma=False)
```

```python
import functools

import jax
import jax.numpy as jnp
from jax import lax
from jax.experimental import pallas as pl
from jax.experimental.pallas import tpu as pltpu
from jax.sharding import PartitionSpec as P

BINS = 32
LAMBDA_REG = 1.0
LANES = 128
GROUP = 4
PER_MESSAGE = 2
PARTS = 4
CHUNK = 2048
SUMS_VMEM = 24 * 2**20
SMALL_VMEM = 4 * 2**20


def cut_sums_kernel(feat_slots, pairs_hbm, codes_hbm, grad_hbm, hess_hbm, out_ref, pairs, codes, grad, hess, grad_wide, hess_wide, sums, code_sems, small_sems):
    groups = feat_slots // GROUP
    first_pair = lax.axis_index("feat") * feat_slots
    row_count = codes.shape[1]
    pairs_copy = pltpu.make_async_copy(pairs_hbm, pairs, small_sems.at[0])
    grad_copy = pltpu.make_async_copy(grad_hbm, grad, small_sems.at[1])
    hess_copy = pltpu.make_async_copy(hess_hbm, hess, small_sems.at[2])
    pairs_copy.start()
    grad_copy.start()
    hess_copy.start()
    pairs_copy.wait()
    code_copies = []
    for slot in range(feat_slots):
        for side in range(2):
            line = 2 * slot + side
            copy = pltpu.make_async_copy(
                codes_hbm.at[pl.ds(pairs[side, first_pair + slot], 1)], codes.at[pl.ds(line, 1)], code_sems.at[line]
            )
            copy.start()
            code_copies.append(copy)
    sums[...] = jnp.zeros_like(sums)
    half = BINS // 2
    levels = lax.broadcasted_iota(jnp.int32, (half, 1), 0).astype(jnp.float32)
    level_parts = (levels.astype(jnp.bfloat16), (levels + half).astype(jnp.bfloat16))
    grad_copy.wait()
    hess_copy.wait()
    for narrow, wide in ((grad, grad_wide), (hess, hess_wide)):
        values = narrow[...].astype(jnp.float32)
        for tile in range(row_count // LANES):
            line = jnp.broadcast_to(values[tile : tile + 1], (half, LANES))
            wide[:, tile * LANES : (tile + 1) * LANES] = line.astype(jnp.bfloat16)
    zero = jnp.zeros((half, CHUNK), jnp.bfloat16)
    one = jnp.ones((half, CHUNK), jnp.bfloat16)
    for copy in code_copies:
        copy.wait()

    def spread(line, span):
        values = codes[pl.ds(line, 1), span].astype(jnp.float32)
        return jnp.broadcast_to(values, (half, CHUNK)).astype(jnp.bfloat16)

    def step(index, carry):
        span = pl.ds(pl.multiple_of(index * CHUNK, CHUNK), CHUNK)
        grad_part = grad_wide[:, span]
        hess_part = hess_wide[:, span]
        for group in range(groups):
            grad_rows, hess_rows, second_rows = [], [], []
            for pair in range(GROUP):
                line = 2 * (GROUP * group + pair)
                first = spread(line, span)
                second = spread(line + 1, span)
                for level in level_parts:
                    below = first <= level
                    grad_rows.append(jnp.where(below, grad_part, zero))
                    hess_rows.append(jnp.where(below, hess_part, zero))
                    second_rows.append(jnp.where(second <= level, one, zero))
            weighted = jnp.concatenate(grad_rows + hess_rows, axis=0)
            hot = jnp.concatenate(second_rows, axis=0)
            sums[group] += lax.dot_general(
                weighted, hot, (((1,), (1,)), ((), ())), preferred_element_type=jnp.float32
            )
        return carry

    lax.fori_loop(0, row_count // CHUNK, step, 0)
    lane = lax.broadcasted_iota(jnp.int32, (BINS, LANES), 1)
    low = lane < LANES // 2

    def own_blocks(group, start):
        block = sums[group, start : start + BINS]
        for pair in range(1, GROUP):
            at = start + pair * BINS
            block = jnp.where(lane >= pair * BINS, sums[group, at : at + BINS], block)
        return block

    for group in range(groups):
        grad_cum = own_blocks(group, 0)
        hess_cum = own_blocks(group, GROUP * BINS)
        out_ref[2 * group] = jnp.where(low, grad_cum, pltpu.roll(hess_cum, LANES // 2, 1))
        out_ref[2 * group + 1] = jnp.where(low, pltpu.roll(grad_cum, LANES // 2, 1), hess_cum)
    for message in range(2 * groups, out_ref.shape[0]):
        out_ref[message] = jnp.zeros((BINS, LANES), jnp.float32)


def cut_sums(bin_codes, gradients, hessians, pair_list, feat_slots, messages):
    row_count = bin_codes.shape[1]
    groups = feat_slots // GROUP
    tiles = row_count // LANES
    anywhere = pl.BlockSpec(memory_space=pl.ANY)
    operands = (pair_list.T, bin_codes, gradients.reshape(tiles, LANES), hessians.reshape(tiles, LANES))
    return pl.pallas_call(
        functools.partial(cut_sums_kernel, feat_slots),
        out_shape=jax.ShapeDtypeStruct((messages, BINS, LANES), jnp.float32),
        in_specs=[anywhere] * 4,
        out_specs=pl.BlockSpec(memory_space=pltpu.VMEM),
        scratch_shapes=[
            pltpu.SMEM((2, pair_list.shape[0]), jnp.int32),
            pltpu.VMEM((2 * feat_slots, row_count), jnp.int32),
            pltpu.VMEM((tiles, LANES), jnp.bfloat16),
            pltpu.VMEM((tiles, LANES), jnp.bfloat16),
            pltpu.VMEM((BINS // 2, row_count), jnp.bfloat16),
            pltpu.VMEM((BINS // 2, row_count), jnp.bfloat16),
            pltpu.VMEM((groups, 2 * GROUP * BINS, GROUP * BINS), jnp.float32),
            pltpu.SemaphoreType.DMA((2 * feat_slots,)),
            pltpu.SemaphoreType.DMA((3,)),
        ],
        compiler_params=pltpu.CompilerParams(vmem_limit_bytes=SUMS_VMEM),
    )(*(pltpu.with_memory_space_constraint(operand, pltpu.HBM) for operand in operands))


def gains_kernel(feat_slots, parts_ref, out_ref, gains):
    row_count, feat_count = out_ref.shape[0], out_ref.shape[1]
    share = BINS // row_count
    total = parts_ref[0]
    for part in range(1, parts_ref.shape[0]):
        total = total + parts_ref[part]
    lane = lax.broadcasted_iota(jnp.int32, (BINS, LANES), 1)
    first_half = lane < BINS

    def ends(cum):
        return jnp.where(first_half, cum[:, BINS - 1 : BINS], cum[:, 2 * BINS - 1 : 2 * BINS])

    grad_cum = total
    hess_cum = pltpu.roll(total, LANES // 2, 1)
    grad_end, hess_end = ends(grad_cum), ends(hess_cum)
    grad_col, hess_col = grad_cum[BINS - 1 :], hess_cum[BINS - 1 :]
    grad_all, hess_all = grad_end[BINS - 1 :], hess_end[BINS - 1 :]
    result = -(grad_all * grad_all) / (hess_all + LAMBDA_REG)
    for grad_part, hess_part in (
        (grad_cum, hess_cum),
        (grad_end - grad_cum, hess_end - hess_cum),
        (grad_col - grad_cum, hess_col - hess_cum),
        (grad_all - grad_end - grad_col + grad_cum, hess_all - hess_end - hess_col + hess_cum),
    ):
        result = result + grad_part * grad_part / (hess_part + LAMBDA_REG)
    gains[...] = result
    peak = jnp.max(result, axis=0, keepdims=True)
    line = lax.broadcasted_iota(jnp.int32, (1, LANES), 1)
    row_index = lax.axis_index("row")
    first_pair = lax.axis_index("feat") * feat_slots + PER_MESSAGE * row_index
    held = row_index < feat_slots // PER_MESSAGE
    best = jnp.zeros((1, LANES), jnp.float32)
    for pair in range(PER_MESSAGE):
        inside = (line >= pair * BINS) & (line < (pair + 1) * BINS)
        top = jnp.max(jnp.where(inside, peak, -jnp.inf), axis=1, keepdims=True)
        best = jnp.where((line == first_pair + pair) & held, top, best)
    wide = lax.broadcasted_iota(jnp.int32, (row_count, LANES), 1)
    cuts = []
    for pair in range(PER_MESSAGE):
        laid = jnp.zeros((row_count, LANES), jnp.float32)
        for step in range(share):
            lines = gains[pl.ds(step, row_count, stride=share), :] if share > 1 else gains[...]
            moved = (step - pair) * BINS % LANES
            if moved:
                lines = pltpu.roll(lines, moved, 1)
            laid = jnp.where((wide >= step * BINS) & (wide < (step + 1) * BINS), lines, laid)
        cuts.append(laid)
    spot = lax.broadcasted_iota(jnp.int32, (PARTS, LANES), 0)
    for row in range(row_count):
        message = jnp.where(spot == 0, cuts[0][row : row + 1], jnp.where(spot == 1, cuts[1][row : row + 1], best))
        for feat in range(feat_count):
            out_ref[row, feat] = message


def table_kernel(feat_slots, feat_count, owners_ref, parts_ref, table_ref, best_ref, table):
    feat_index = lax.axis_index("feat")
    home_slots, width = table_ref.shape
    table[...] = jnp.zeros_like(table)
    taken = jnp.int32(0)
    for pair in range(owners_ref.shape[0]):
        place = pair % feat_slots
        source = place // PER_MESSAGE * feat_count + pair // feat_slots
        mine = owners_ref[pair] == feat_index
        slot = jnp.where(mine, jnp.minimum(taken, home_slots), home_slots)
        table[pl.ds(slot, 1), :] = parts_ref[source, place % PER_MESSAGE : place % PER_MESSAGE + 1, :]
        taken = taken + mine.astype(jnp.int32)
    table_ref[...] = table[:home_slots, :width]
    best = jnp.sum(parts_ref[:, PER_MESSAGE, :], axis=0, keepdims=True)
    best_ref[...] = best[:, : best_ref.shape[1]]


def shards(bin_codes, gradients, hessians, pair_list, owners):
    feat_count = lax.axis_size("feat")
    row_count = lax.axis_size("row")
    pair_count = pair_list.shape[0]
    feat_slots = pair_count // feat_count
    home_slots = 2 * pair_count // feat_count
    width = BINS // row_count * BINS
    in_vmem = pl.BlockSpec(memory_space=pltpu.VMEM)
    partial = cut_sums(bin_codes, gradients, hessians, pair_list, feat_slots, row_count)
    parts = lax.all_to_all(partial, "row", split_axis=0, concat_axis=0, tiled=True)
    outgoing = pl.pallas_call(
        functools.partial(gains_kernel, feat_slots),
        out_shape=jax.ShapeDtypeStruct((row_count, feat_count, PARTS, LANES), jnp.float32),
        in_specs=[in_vmem],
        out_specs=in_vmem,
        scratch_shapes=[pltpu.VMEM((BINS, LANES), jnp.float32)],
        compiler_params=pltpu.CompilerParams(vmem_limit_bytes=SMALL_VMEM),
    )(parts)
    outgoing = outgoing.reshape(row_count * feat_count, PARTS, LANES)
    incoming = lax.all_to_all(outgoing, ("row", "feat"), split_axis=0, concat_axis=0, tiled=True)
    cut_table, best = pl.pallas_call(
        functools.partial(table_kernel, feat_slots, feat_count),
        out_shape=(
            jax.ShapeDtypeStruct((home_slots, width), jnp.float32),
            jax.ShapeDtypeStruct((1, pair_count), jnp.float32),
        ),
        in_specs=[pl.BlockSpec(memory_space=pltpu.SMEM), in_vmem],
        out_specs=(in_vmem, in_vmem),
        scratch_shapes=[pltpu.VMEM((home_slots + 8, LANES), jnp.float32)],
        compiler_params=pltpu.CompilerParams(vmem_limit_bytes=SMALL_VMEM),
    )(owners, incoming)
    return (cut_table, best.reshape(pair_count))


def solution(mesh):
    in_specs = (P(None, "row"), P("row"), P("row"), P(), P())
    out_specs = (P("feat", "row"), P())
    return jax.shard_map(shards, mesh=mesh, in_specs=in_specs, out_specs=out_specs, check_vma=False)
```

```python
import functools

import jax
import jax.numpy as jnp
from jax import lax
from jax.experimental import pallas as pl
from jax.experimental.pallas import tpu as pltpu
from jax.sharding import PartitionSpec as P

BINS = 32
LAMBDA_REG = 1.0
LANES = 128
GROUP = 4
PER_MESSAGE = 2
PARTS = 4
CHUNK = 4096
SUMS_VMEM = 40 * 2**20
SMALL_VMEM = 4 * 2**20


def cut_sums_kernel(feat_slots, pairs_hbm, codes_hbm, grad_hbm, hess_hbm, out_ref, pairs, codes, grad, hess, grad_tall, hess_tall, sums, code_sems, small_sems):
    groups = feat_slots // GROUP
    first_pair = lax.axis_index("feat") * feat_slots
    row_count = codes.shape[1]
    chunks = row_count // CHUNK
    pairs_copy = pltpu.make_async_copy(pairs_hbm, pairs, small_sems.at[0])
    grad_copy = pltpu.make_async_copy(grad_hbm, grad, small_sems.at[1])
    hess_copy = pltpu.make_async_copy(hess_hbm, hess, small_sems.at[2])
    pairs_copy.start()
    grad_copy.start()
    hess_copy.start()
    pairs_copy.wait()

    def code_copy(feature, line):
        return pltpu.make_async_copy(
            codes_hbm.at[pl.ds(feature, 1)], codes.at[pl.ds(line, 1)], code_sems.at[line]
        )

    code_copies = []
    for line in range(2 * feat_slots):
        copy = code_copy(pairs[line % 2, first_pair + line // 2], line)
        copy.start()
        code_copies.append(copy)
    sums[...] = jnp.zeros_like(sums)
    half = BINS // 2
    levels = lax.broadcasted_iota(jnp.int32, (half, 1), 0).astype(jnp.float32)
    level_parts = (levels.astype(jnp.bfloat16), (levels + half).astype(jnp.bfloat16))
    grad_copy.wait()
    hess_copy.wait()
    for flat, tall in ((grad, grad_tall), (hess, hess_tall)):
        values = flat[...].astype(jnp.float32)
        for tile in range(row_count // LANES):
            square = jnp.broadcast_to(values[tile : tile + 1], (LANES, LANES)).astype(jnp.bfloat16)
            tall[tile * LANES : (tile + 1) * LANES, :] = square.T
    zero = jnp.zeros((half, CHUNK), jnp.bfloat16)
    one = jnp.ones((half, CHUNK), jnp.bfloat16)

    def below(line, span):
        values = codes[pl.ds(line, 1), span].astype(jnp.float32)
        values = jnp.broadcast_to(values, (half, CHUNK)).astype(jnp.bfloat16)
        return [jnp.where(values <= level, one, zero) for level in level_parts]

    for copy in code_copies:
        copy.wait()

    def step(chunk, carry):
        span = pl.ds(pl.multiple_of(chunk * CHUNK, CHUNK), CHUNK)
        grad_part = grad_tall[span, :]
        hess_part = hess_tall[span, :]
        for group in range(groups):
            first_rows, second_rows = [], []
            for pair in range(GROUP):
                line = 2 * (GROUP * group + pair)
                first_rows += below(line, span)
                second_rows += below(line + 1, span)
            first = jnp.concatenate(first_rows, axis=0)
            second = jnp.concatenate(second_rows, axis=0).T
            weighted = jnp.concatenate([second * grad_part, second * hess_part], axis=1)
            sums[group] += jnp.dot(first, weighted, preferred_element_type=jnp.float32)
        return carry

    lax.fori_loop(0, chunks, step, 0)
    lane = lax.broadcasted_iota(jnp.int32, (BINS, LANES), 1)
    low = lane < LANES // 2

    def own_blocks(group, start):
        block = sums[group, :BINS, start : start + LANES]
        for pair in range(1, GROUP):
            at = pair * BINS
            block = jnp.where(lane >= at, sums[group, at : at + BINS, start : start + LANES], block)
        return block

    for group in range(groups):
        grad_cum = own_blocks(group, 0)
        hess_cum = own_blocks(group, LANES)
        out_ref[2 * group] = jnp.where(low, grad_cum, pltpu.roll(hess_cum, LANES // 2, 1))
        out_ref[2 * group + 1] = jnp.where(low, pltpu.roll(grad_cum, LANES // 2, 1), hess_cum)
    for message in range(2 * groups, out_ref.shape[0]):
        out_ref[message] = jnp.zeros((BINS, LANES), jnp.float32)


def cut_sums(bin_codes, gradients, hessians, pair_list, feat_slots, messages):
    row_count = bin_codes.shape[1]
    groups = feat_slots // GROUP
    tiles = row_count // LANES
    anywhere = pl.BlockSpec(memory_space=pl.ANY)
    operands = (pair_list.T, bin_codes, gradients.reshape(tiles, LANES), hessians.reshape(tiles, LANES))
    return pl.pallas_call(
        functools.partial(cut_sums_kernel, feat_slots),
        out_shape=jax.ShapeDtypeStruct((messages, BINS, LANES), jnp.float32),
        in_specs=[anywhere] * 4,
        out_specs=pl.BlockSpec(memory_space=pltpu.VMEM),
        scratch_shapes=[
            pltpu.SMEM((2, pair_list.shape[0]), jnp.int32),
            pltpu.VMEM((2 * feat_slots, row_count), jnp.int32),
            pltpu.VMEM((tiles, LANES), jnp.bfloat16),
            pltpu.VMEM((tiles, LANES), jnp.bfloat16),
            pltpu.VMEM((row_count, LANES), jnp.bfloat16),
            pltpu.VMEM((row_count, LANES), jnp.bfloat16),
            pltpu.VMEM((groups, GROUP * BINS, 2 * GROUP * BINS), jnp.float32),
            pltpu.SemaphoreType.DMA((2 * feat_slots,)),
            pltpu.SemaphoreType.DMA((3,)),
        ],
        compiler_params=pltpu.CompilerParams(vmem_limit_bytes=SUMS_VMEM),
    )(*(pltpu.with_memory_space_constraint(operand, pltpu.HBM) for operand in operands))


def gains_kernel(feat_slots, parts_ref, out_ref, gains):
    row_count, feat_count = out_ref.shape[0], out_ref.shape[1]
    share = BINS // row_count
    total = parts_ref[0]
    for part in range(1, parts_ref.shape[0]):
        total = total + parts_ref[part]
    lane = lax.broadcasted_iota(jnp.int32, (BINS, LANES), 1)
    first_half = lane < BINS

    def ends(cum):
        return jnp.where(first_half, cum[:, BINS - 1 : BINS], cum[:, 2 * BINS - 1 : 2 * BINS])

    grad_cum = total
    hess_cum = pltpu.roll(total, LANES // 2, 1)
    grad_end, hess_end = ends(grad_cum), ends(hess_cum)
    grad_col, hess_col = grad_cum[BINS - 1 :], hess_cum[BINS - 1 :]
    grad_all, hess_all = grad_end[BINS - 1 :], hess_end[BINS - 1 :]
    result = -(grad_all * grad_all) / (hess_all + LAMBDA_REG)
    for grad_part, hess_part in (
        (grad_cum, hess_cum),
        (grad_end - grad_cum, hess_end - hess_cum),
        (grad_col - grad_cum, hess_col - hess_cum),
        (grad_all - grad_end - grad_col + grad_cum, hess_all - hess_end - hess_col + hess_cum),
    ):
        result = result + grad_part * grad_part / (hess_part + LAMBDA_REG)
    gains[...] = result
    peak = jnp.max(result, axis=0, keepdims=True)
    line = lax.broadcasted_iota(jnp.int32, (1, LANES), 1)
    row_index = lax.axis_index("row")
    first_pair = lax.axis_index("feat") * feat_slots + PER_MESSAGE * row_index
    held = row_index < feat_slots // PER_MESSAGE
    best = jnp.zeros((1, LANES), jnp.float32)
    for pair in range(PER_MESSAGE):
        inside = (line >= pair * BINS) & (line < (pair + 1) * BINS)
        top = jnp.max(jnp.where(inside, peak, -jnp.inf), axis=1, keepdims=True)
        best = jnp.where((line == first_pair + pair) & held, top, best)
    wide = lax.broadcasted_iota(jnp.int32, (row_count, LANES), 1)
    cuts = []
    for pair in range(PER_MESSAGE):
        laid = jnp.zeros((row_count, LANES), jnp.float32)
        for step in range(share):
            lines = gains[pl.ds(step, row_count, stride=share), :] if share > 1 else gains[...]
            moved = (step - pair) * BINS % LANES
            if moved:
                lines = pltpu.roll(lines, moved, 1)
            laid = jnp.where((wide >= step * BINS) & (wide < (step + 1) * BINS), lines, laid)
        cuts.append(laid)
    spot = lax.broadcasted_iota(jnp.int32, (PARTS, LANES), 0)
    for row in range(row_count):
        message = jnp.where(spot == 0, cuts[0][row : row + 1], jnp.where(spot == 1, cuts[1][row : row + 1], best))
        for feat in range(feat_count):
            out_ref[row, feat] = message


def table_kernel(feat_slots, feat_count, owners_ref, parts_ref, table_ref, best_ref, table):
    feat_index = lax.axis_index("feat")
    home_slots, width = table_ref.shape
    table[...] = jnp.zeros_like(table)
    taken = jnp.int32(0)
    for pair in range(owners_ref.shape[0]):
        place = pair % feat_slots
        source = place // PER_MESSAGE * feat_count + pair // feat_slots
        mine = owners_ref[pair] == feat_index
        slot = jnp.where(mine, jnp.minimum(taken, home_slots), home_slots)
        table[pl.ds(slot, 1), :] = parts_ref[source, place % PER_MESSAGE : place % PER_MESSAGE + 1, :]
        taken = taken + mine.astype(jnp.int32)
    table_ref[...] = table[:home_slots, :width]
    best = jnp.sum(parts_ref[:, PER_MESSAGE, :], axis=0, keepdims=True)
    best_ref[...] = best[:, : best_ref.shape[1]]


def shards(bin_codes, gradients, hessians, pair_list, owners):
    feat_count = lax.axis_size("feat")
    row_count = lax.axis_size("row")
    pair_count = pair_list.shape[0]
    feat_slots = pair_count // feat_count
    home_slots = 2 * pair_count // feat_count
    width = BINS // row_count * BINS
    in_vmem = pl.BlockSpec(memory_space=pltpu.VMEM)
    partial = cut_sums(bin_codes, gradients, hessians, pair_list, feat_slots, row_count)
    parts = lax.all_to_all(partial, "row", split_axis=0, concat_axis=0, tiled=True)
    outgoing = pl.pallas_call(
        functools.partial(gains_kernel, feat_slots),
        out_shape=jax.ShapeDtypeStruct((row_count, feat_count, PARTS, LANES), jnp.float32),
        in_specs=[in_vmem],
        out_specs=in_vmem,
        scratch_shapes=[pltpu.VMEM((BINS, LANES), jnp.float32)],
        compiler_params=pltpu.CompilerParams(vmem_limit_bytes=SMALL_VMEM),
    )(parts)
    outgoing = outgoing.reshape(row_count * feat_count, PARTS, LANES)
    incoming = lax.all_to_all(outgoing, ("row", "feat"), split_axis=0, concat_axis=0, tiled=True)
    cut_table, best = pl.pallas_call(
        functools.partial(table_kernel, feat_slots, feat_count),
        out_shape=(
            jax.ShapeDtypeStruct((home_slots, width), jnp.float32),
            jax.ShapeDtypeStruct((1, pair_count), jnp.float32),
        ),
        in_specs=[pl.BlockSpec(memory_space=pltpu.SMEM), in_vmem],
        out_specs=(in_vmem, in_vmem),
        scratch_shapes=[pltpu.VMEM((home_slots + 8, LANES), jnp.float32)],
        compiler_params=pltpu.CompilerParams(vmem_limit_bytes=SMALL_VMEM),
    )(owners, incoming)
    return (cut_table, best.reshape(pair_count))


def solution(mesh):
    in_specs = (P(None, "row"), P("row"), P("row"), P(), P())
    out_specs = (P("feat", "row"), P())
    return jax.shard_map(shards, mesh=mesh, in_specs=in_specs, out_specs=out_specs, check_vma=False)
```

```python
import functools

import jax
import jax.numpy as jnp
from jax import lax
from jax.experimental import pallas as pl
from jax.experimental.pallas import tpu as pltpu
from jax.sharding import PartitionSpec as P

BINS = 32
LAMBDA_REG = 1.0
LANES = 128
GROUP = 4
PER_MESSAGE = 2
PARTS = 4
CHUNK = 4096
SUMS_VMEM = 40 * 2**20
SMALL_VMEM = 4 * 2**20


def route_tables(feat_slots, lines, pair_count):
    feat_count = pair_count // feat_slots
    row = lax.broadcasted_iota(jnp.int32, (pair_count, lines), 1)
    source, part = row // PARTS, row % PARTS
    place = source // feat_count * PER_MESSAGE + part
    pair = source % feat_count * feat_slots + place
    held = (part < PER_MESSAGE) & (place < feat_slots)
    holders = held & (pair == lax.broadcasted_iota(jnp.int32, (pair_count, lines), 0))
    square = (pair_count, pair_count)
    earlier = lax.broadcasted_iota(jnp.int32, square, 0) < lax.broadcasted_iota(jnp.int32, square, 1)
    return holders.astype(jnp.float32), earlier.astype(jnp.float32)


def route(mine, holders, earlier, home_slots, shape):
    owned = jnp.broadcast_to(mine.astype(jnp.float32), (8, mine.shape[1]))
    rank = jnp.dot(owned, earlier, preferred_element_type=jnp.float32)
    upper = lax.broadcasted_iota(jnp.int32, owned.shape, 0) == 0
    spread = jnp.dot(jnp.where(upper, owned, rank), holders, preferred_element_type=jnp.float32)
    slot = lax.broadcasted_iota(jnp.int32, shape, 0)
    taken = jnp.where(spread[1:2].astype(jnp.int32) == slot, spread[0:1], 0.0)
    best_row = jnp.where(lax.broadcasted_iota(jnp.int32, shape, 1) % PARTS == PER_MESSAGE, 1.0, 0.0)
    return jnp.where(slot < home_slots, taken, best_row)


def cut_sums_kernel(
    feat_slots, home_slots, pairs_hbm, codes_hbm, grad_hbm, hess_hbm, owners_hbm, out_ref, route_ref,
    pairs, codes, grad, hess, owners, grad_tall, hess_tall, sums, code_sem, small_sems,
):
    groups = feat_slots // GROUP
    feat_index = lax.axis_index("feat")
    first_pair = feat_index * feat_slots
    row_count = codes.shape[1]
    chunks = row_count // CHUNK
    pairs_copy = pltpu.make_async_copy(pairs_hbm, pairs, small_sems.at[0])
    grad_copy = pltpu.make_async_copy(grad_hbm, grad, small_sems.at[1])
    hess_copy = pltpu.make_async_copy(hess_hbm, hess, small_sems.at[2])
    owners_copy = pltpu.make_async_copy(owners_hbm, owners, small_sems.at[3])
    pairs_copy.start()
    grad_copy.start()
    hess_copy.start()
    owners_copy.start()
    sums[...] = jnp.zeros_like(sums)
    holders, earlier = route_tables(feat_slots, route_ref.shape[1], owners.shape[1])
    pairs_copy.wait()

    for line in range(2 * feat_slots):
        feature = pairs[line % 2, first_pair + line // 2]
        pltpu.make_async_copy(codes_hbm.at[pl.ds(feature, 1)], codes.at[pl.ds(line, 1)], code_sem).start()
    half = BINS // 2
    levels = lax.broadcasted_iota(jnp.int32, (half, 1), 0).astype(jnp.float32)
    level_parts = (levels.astype(jnp.bfloat16), (levels + half).astype(jnp.bfloat16))
    grad_copy.wait()
    hess_copy.wait()
    owners_copy.wait()
    route_ref[...] = route(owners[...] == feat_index, holders, earlier, home_slots, route_ref.shape)
    for flat, tall in ((grad, grad_tall), (hess, hess_tall)):
        values = flat[...].astype(jnp.float32)
        for tile in range(row_count // LANES):
            square = jnp.broadcast_to(values[tile : tile + 1], (LANES, LANES)).astype(jnp.bfloat16)
            tall[tile * LANES : (tile + 1) * LANES, :] = square.T
    zero = jnp.zeros((half, CHUNK), jnp.bfloat16)
    one = jnp.ones((half, CHUNK), jnp.bfloat16)

    def below(line, span):
        values = codes[pl.ds(line, 1), span].astype(jnp.float32)
        values = jnp.broadcast_to(values, (half, CHUNK)).astype(jnp.bfloat16)
        return [jnp.where(values <= level, one, zero) for level in level_parts]

    pltpu.make_async_copy(codes_hbm.at[pl.ds(0, 2 * feat_slots)], codes, code_sem).wait()

    def step(chunk, carry):
        span = pl.ds(pl.multiple_of(chunk * CHUNK, CHUNK), CHUNK)
        grad_part = grad_tall[span, :]
        hess_part = hess_tall[span, :]
        for group in range(groups):
            first_rows, second_rows = [], []
            for pair in range(GROUP):
                line = 2 * (GROUP * group + pair)
                first_rows += below(line, span)
                second_rows += below(line + 1, span)
            first = jnp.concatenate(first_rows, axis=0)
            second = jnp.concatenate(second_rows, axis=0).T
            weighted = jnp.concatenate([second * grad_part, second * hess_part], axis=1)
            sums[group] += jnp.dot(first, weighted, preferred_element_type=jnp.float32)
        return carry

    lax.fori_loop(0, chunks, step, 0)
    lane = lax.broadcasted_iota(jnp.int32, (BINS, LANES), 1)
    low = lane < LANES // 2

    def own_blocks(group, start):
        block = sums[group, :BINS, start : start + LANES]
        for pair in range(1, GROUP):
            at = pair * BINS
            block = jnp.where(lane >= at, sums[group, at : at + BINS, start : start + LANES], block)
        return block

    for group in range(groups):
        grad_cum = own_blocks(group, 0)
        hess_cum = own_blocks(group, LANES)
        out_ref[2 * group] = jnp.where(low, grad_cum, pltpu.roll(hess_cum, LANES // 2, 1))
        out_ref[2 * group + 1] = jnp.where(low, pltpu.roll(grad_cum, LANES // 2, 1), hess_cum)
    for message in range(2 * groups, out_ref.shape[0]):
        out_ref[message] = jnp.zeros((BINS, LANES), jnp.float32)


def cut_sums(bin_codes, gradients, hessians, pair_list, owners, feat_slots, messages):
    row_count = bin_codes.shape[1]
    groups = feat_slots // GROUP
    tiles = row_count // LANES
    pair_count = owners.shape[0]
    feat_count = pair_count // feat_slots
    home_slots = 2 * feat_slots
    anywhere = pl.BlockSpec(memory_space=pl.ANY)
    in_vmem = pl.BlockSpec(memory_space=pltpu.VMEM)
    flat = (gradients.reshape(tiles, LANES), hessians.reshape(tiles, LANES), owners.reshape(1, pair_count))
    operands = (pair_list.T, bin_codes) + flat
    return pl.pallas_call(
        functools.partial(cut_sums_kernel, feat_slots, home_slots),
        out_shape=(
            jax.ShapeDtypeStruct((messages, BINS, LANES), jnp.float32),
            jax.ShapeDtypeStruct((home_slots + 8, messages * feat_count * PARTS), jnp.float32),
        ),
        in_specs=[anywhere] * 5,
        out_specs=(in_vmem, in_vmem),
        scratch_shapes=[
            pltpu.SMEM((2, pair_count), jnp.int32),
            pltpu.VMEM((2 * feat_slots, row_count), jnp.int32),
            pltpu.VMEM((tiles, LANES), jnp.bfloat16),
            pltpu.VMEM((tiles, LANES), jnp.bfloat16),
            pltpu.VMEM((1, pair_count), jnp.int32),
            pltpu.VMEM((row_count, LANES), jnp.bfloat16),
            pltpu.VMEM((row_count, LANES), jnp.bfloat16),
            pltpu.VMEM((groups, GROUP * BINS, 2 * GROUP * BINS), jnp.float32),
            pltpu.SemaphoreType.DMA,
            pltpu.SemaphoreType.DMA((4,)),
        ],
        compiler_params=pltpu.CompilerParams(vmem_limit_bytes=SUMS_VMEM),
    )(*(pltpu.with_memory_space_constraint(operand, pltpu.HBM) for operand in operands))


def gains_kernel(feat_slots, parts_ref, out_ref, gains):
    row_count, feat_count = out_ref.shape[0], out_ref.shape[1]
    share = BINS // row_count
    total = parts_ref[0]
    for part in range(1, parts_ref.shape[0]):
        total = total + parts_ref[part]
    lane = lax.broadcasted_iota(jnp.int32, (BINS, LANES), 1)
    first_half = lane < BINS

    def ends(cum):
        return jnp.where(first_half, cum[:, BINS - 1 : BINS], cum[:, 2 * BINS - 1 : 2 * BINS])

    grad_cum = total
    hess_cum = pltpu.roll(total, LANES // 2, 1)
    grad_end, hess_end = ends(grad_cum), ends(hess_cum)
    grad_col, hess_col = grad_cum[BINS - 1 :], hess_cum[BINS - 1 :]
    grad_all, hess_all = grad_end[BINS - 1 :], hess_end[BINS - 1 :]
    result = -(grad_all * grad_all) / (hess_all + LAMBDA_REG)
    for grad_part, hess_part in (
        (grad_cum, hess_cum),
        (grad_end - grad_cum, hess_end - hess_cum),
        (grad_col - grad_cum, hess_col - hess_cum),
        (grad_all - grad_end - grad_col + grad_cum, hess_all - hess_end - hess_col + hess_cum),
    ):
        result = result + grad_part * grad_part / (hess_part + LAMBDA_REG)
    gains[...] = result
    peak = jnp.max(result, axis=0, keepdims=True)
    line = lax.broadcasted_iota(jnp.int32, (1, LANES), 1)
    row_index = lax.axis_index("row")
    first_pair = lax.axis_index("feat") * feat_slots + PER_MESSAGE * row_index
    held = row_index < feat_slots // PER_MESSAGE
    best = jnp.zeros((1, LANES), jnp.float32)
    for pair in range(PER_MESSAGE):
        inside = (line >= pair * BINS) & (line < (pair + 1) * BINS)
        top = jnp.max(jnp.where(inside, peak, -jnp.inf), axis=1, keepdims=True)
        best = jnp.where((line == first_pair + pair) & held, top, best)
    wide = lax.broadcasted_iota(jnp.int32, (row_count, LANES), 1)
    cuts = []
    for pair in range(PER_MESSAGE):
        laid = jnp.zeros((row_count, LANES), jnp.float32)
        for step in range(share):
            lines = gains[pl.ds(step, row_count, stride=share), :] if share > 1 else gains[...]
            moved = (step - pair) * BINS % LANES
            if moved:
                lines = pltpu.roll(lines, moved, 1)
            laid = jnp.where((wide >= step * BINS) & (wide < (step + 1) * BINS), lines, laid)
        cuts.append(laid)
    spot = lax.broadcasted_iota(jnp.int32, (PARTS, LANES), 0)
    for row in range(row_count):
        message = jnp.where(spot == 0, cuts[0][row : row + 1], jnp.where(spot == 1, cuts[1][row : row + 1], best))
        for feat in range(feat_count):
            out_ref[row, feat] = message


def table_kernel(route_ref, parts_ref, table_hbm, best_hbm, table, best, sems):
    ways = route_ref[...].astype(jnp.bfloat16)
    rest = parts_ref[...]
    placed = jnp.zeros(route_ref.shape[:1] + rest.shape[1:], jnp.float32)
    for _ in range(3):
        part = rest.astype(jnp.bfloat16)
        rest = rest - part.astype(jnp.float32)
        placed = placed + jnp.dot(ways, part, preferred_element_type=jnp.float32)
    home_slots, width = table.shape
    table[...] = placed[:home_slots, :width]
    best[...] = placed[home_slots : home_slots + 1, : best.shape[1]]
    copies = (
        pltpu.make_async_copy(table, table_hbm, sems.at[0]),
        pltpu.make_async_copy(best, best_hbm, sems.at[1]),
    )
    for copy in copies:
        copy.start()
    for copy in copies:
        copy.wait()


def shards(bin_codes, gradients, hessians, pair_list, owners):
    feat_count = lax.axis_size("feat")
    row_count = lax.axis_size("row")
    pair_count = pair_list.shape[0]
    feat_slots = pair_count // feat_count
    home_slots = 2 * pair_count // feat_count
    width = BINS // row_count * BINS
    in_vmem = pl.BlockSpec(memory_space=pltpu.VMEM)
    partial, ways = cut_sums(bin_codes, gradients, hessians, pair_list, owners, feat_slots, row_count)
    parts = lax.all_to_all(partial, "row", split_axis=0, concat_axis=0, tiled=True)
    outgoing = pl.pallas_call(
        functools.partial(gains_kernel, feat_slots),
        out_shape=jax.ShapeDtypeStruct((row_count, feat_count, PARTS, LANES), jnp.float32),
        in_specs=[in_vmem],
        out_specs=in_vmem,
        scratch_shapes=[pltpu.VMEM((BINS, LANES), jnp.float32)],
        compiler_params=pltpu.CompilerParams(vmem_limit_bytes=SMALL_VMEM),
    )(parts)
    outgoing = outgoing.reshape(row_count * feat_count, PARTS, LANES)
    incoming = lax.all_to_all(outgoing, ("row", "feat"), split_axis=0, concat_axis=0, tiled=True)
    incoming = incoming.reshape(row_count * feat_count * PARTS, LANES)
    anywhere = pl.BlockSpec(memory_space=pl.ANY)
    cut_table, best = pl.pallas_call(
        table_kernel,
        out_shape=(
            jax.ShapeDtypeStruct((home_slots, width), jnp.float32),
            jax.ShapeDtypeStruct((1, pair_count), jnp.float32),
        ),
        in_specs=[in_vmem, in_vmem],
        out_specs=(anywhere, anywhere),
        scratch_shapes=[
            pltpu.VMEM((home_slots, width), jnp.float32),
            pltpu.VMEM((1, pair_count), jnp.float32),
            pltpu.SemaphoreType.DMA((2,)),
        ],
        compiler_params=pltpu.CompilerParams(vmem_limit_bytes=SMALL_VMEM),
    )(ways, incoming)
    return (cut_table, best.reshape(pair_count))


def solution(mesh):
    in_specs = (P(None, "row"), P("row"), P("row"), P(), P())
    out_specs = (P("feat", "row"), P())
    return jax.shard_map(shards, mesh=mesh, in_specs=in_specs, out_specs=out_specs, check_vma=False)
```

```python
import functools

import jax
import jax.numpy as jnp
from jax import lax
from jax.experimental import pallas as pl
from jax.experimental.pallas import tpu as pltpu
from jax.sharding import PartitionSpec as P

BINS = 32
LAMBDA_REG = 1.0
LANES = 128
CORES = 2
GROUP = 4
HALF = BINS // 2
PARTS = 4
CHUNK = 4096
HEAD = 5
LATE_HEAD = 5
SUMS_VMEM = 40 * 2**20
SMALL_VMEM = 4 * 2**20


class Plan:
    def __init__(self, row_count, feat_count, pair_count):
        self.row_count = row_count
        self.pair_count = pair_count
        self.chips = feat_count // CORES
        self.chip_pairs = pair_count // self.chips
        self.home_slots = 2 * pair_count // feat_count
        light = self.chip_pairs // GROUP // 4 * GROUP
        self.start = (0, light)
        self.count = (light, self.chip_pairs - light)
        self.per = tuple(-(-count // row_count) for count in self.count)
        self.head = HEAD * row_count // 8
        self.rows = [self.head] + [row for row in range(row_count) if row != self.head]
        self.members = row_count * self.chips
        self.late_head = LATE_HEAD * row_count // 8 * self.chips + self.chips - 1
        self.order = [self.late_head] + [member for member in range(self.members) if member != self.late_head]


def seat(member, head):
    return jnp.where(member == head, 0, jnp.where(member < head, member + 1, member))


def sitter(place, head):
    return jnp.where(place == 0, head, jnp.where(place <= head, place - 1, place))


def route_tables(plan):
    shape = (plan.pair_count, CORES * plan.members * PARTS)
    spot = lax.broadcasted_iota(jnp.int32, shape, 1)
    part, seated, other = spot % PARTS, spot // PARTS % plan.members, spot // (PARTS * plan.members)
    device = sitter(seated, plan.late_head)
    light = (lax.axis_index("feat") + other) % CORES == 0
    per, start, count = (jnp.where(light, values[0], values[1]) for values in (plan.per, plan.start, plan.count))
    place = seat(device // plan.chips, plan.head) * per + part
    pair = device % plan.chips * plan.chip_pairs + start + place
    held = (part < per) & (place < count)
    holders = held & (pair == lax.broadcasted_iota(jnp.int32, shape, 0))
    square = (plan.pair_count, plan.pair_count)
    earlier = lax.broadcasted_iota(jnp.int32, square, 0) < lax.broadcasted_iota(jnp.int32, square, 1)
    return holders.astype(jnp.float32), earlier.astype(jnp.float32)


def route(mine, holders, earlier, home_slots, shape):
    owned = jnp.broadcast_to(mine.astype(jnp.float32), (8, mine.shape[1]))
    rank = jnp.dot(owned, earlier, preferred_element_type=jnp.float32)
    upper = lax.broadcasted_iota(jnp.int32, owned.shape, 0) == 0
    spread = jnp.dot(jnp.where(upper, owned, rank), holders, preferred_element_type=jnp.float32)
    slot = lax.broadcasted_iota(jnp.int32, shape, 0)
    taken = jnp.where(spread[1:2].astype(jnp.int32) == slot, spread[0:1], 0.0)
    best_row = jnp.where(lax.broadcasted_iota(jnp.int32, shape, 1) % PARTS == PARTS - 1, 1.0, 0.0)
    return jnp.where(slot < home_slots, taken, best_row)


def cut_sums_kernel(
    plan, start, count, per, pairs_hbm, codes_hbm, grad_hbm, hess_hbm, owners_hbm, out_ref, route_ref,
    pairs, codes, grad, hess, owners, grad_tall, hess_tall, sums, code_sem, small_sems,
):
    groups = count // GROUP
    row_messages = out_ref.shape[0]
    feat_index = lax.axis_index("feat")
    first_pair = feat_index // CORES * plan.chip_pairs + start
    row_count = codes.shape[1]
    chunks = row_count // CHUNK
    pairs_copy = pltpu.make_async_copy(pairs_hbm, pairs, small_sems.at[0])
    grad_copy = pltpu.make_async_copy(grad_hbm, grad, small_sems.at[1])
    hess_copy = pltpu.make_async_copy(hess_hbm, hess, small_sems.at[2])
    owners_copy = pltpu.make_async_copy(owners_hbm, owners, small_sems.at[3])
    pairs_copy.start()
    grad_copy.start()
    hess_copy.start()
    owners_copy.start()
    sums[...] = jnp.zeros_like(sums)
    holders, earlier = route_tables(plan)
    pairs_copy.wait()

    for line in range(2 * count):
        feature = pairs[line % 2, first_pair + line // 2]
        pltpu.make_async_copy(codes_hbm.at[pl.ds(feature, 1)], codes.at[pl.ds(line, 1)], code_sem).start()
    levels = lax.broadcasted_iota(jnp.int32, (HALF, 1), 0).astype(jnp.float32)
    level_parts = (levels.astype(jnp.bfloat16), (levels + HALF).astype(jnp.bfloat16))
    grad_copy.wait()
    hess_copy.wait()
    owners_copy.wait()
    route_ref[...] = route(owners[...] == feat_index, holders, earlier, plan.home_slots, route_ref.shape)
    for flat, tall in ((grad, grad_tall), (hess, hess_tall)):
        values = flat[...].astype(jnp.float32)
        for tile in range(row_count // LANES):
            square = jnp.broadcast_to(values[tile : tile + 1], (LANES, LANES)).astype(jnp.bfloat16)
            tall[tile * LANES : (tile + 1) * LANES, :] = square.T
    zero = jnp.zeros((HALF, CHUNK), jnp.bfloat16)
    one = jnp.ones((HALF, CHUNK), jnp.bfloat16)

    def below(line, span):
        values = codes[pl.ds(line, 1), span].astype(jnp.float32)
        values = jnp.broadcast_to(values, (HALF, CHUNK)).astype(jnp.bfloat16)
        return [jnp.where(values <= level, one, zero) for level in level_parts]

    pltpu.make_async_copy(codes_hbm.at[pl.ds(0, 2 * count)], codes, code_sem).wait()

    def step(chunk, carry):
        span = pl.ds(pl.multiple_of(chunk * CHUNK, CHUNK), CHUNK)
        grad_part = grad_tall[span, :]
        hess_part = hess_tall[span, :]
        for group in range(groups):
            first_rows, second_rows = [], []
            for pair in range(GROUP):
                line = 2 * (GROUP * group + pair)
                first_rows += below(line, span)
                second_rows += below(line + 1, span)
            first = jnp.concatenate(first_rows, axis=0)
            second = jnp.concatenate(second_rows, axis=0).T
            weighted = jnp.concatenate([second * grad_part, second * hess_part], axis=1)
            sums[group] += jnp.dot(first, weighted, preferred_element_type=jnp.float32)
        return carry

    lax.fori_loop(0, chunks, step, 0)
    lane = lax.broadcasted_iota(jnp.int32, (HALF, LANES), 1)
    for place in range(row_messages * per):
        message, at = place // per, place % per * HALF
        if place >= count:
            out_ref[message, at : at + HALF] = jnp.zeros((HALF, LANES), jnp.float32)
            continue
        group, pair = place // GROUP, place % GROUP
        block = None
        for quarter in range(4):
            top, left = pair * BINS + quarter // 2 * HALF, quarter % 2 * LANES
            piece = sums[group, top : top + HALF, left : left + LANES]
            moved = (quarter - pair) * BINS % LANES
            if moved:
                piece = pltpu.roll(piece, moved, 1)
            block = piece if block is None else jnp.where(lane >= quarter * BINS, piece, block)
        out_ref[message, at : at + HALF] = block


def cut_sums(plan, core, bin_codes, gradients, hessians, pair_list, owners):
    row_count = bin_codes.shape[1]
    start, count, per = plan.start[core], plan.count[core], plan.per[core]
    groups = count // GROUP
    tiles = row_count // LANES
    anywhere = pl.BlockSpec(memory_space=pl.ANY)
    in_vmem = pl.BlockSpec(memory_space=pltpu.VMEM)
    flat = (gradients.reshape(tiles, LANES), hessians.reshape(tiles, LANES), owners.reshape(1, plan.pair_count))
    operands = (pair_list.T, bin_codes) + flat
    return pl.pallas_call(
        functools.partial(cut_sums_kernel, plan, start, count, per),
        out_shape=(
            jax.ShapeDtypeStruct((plan.row_count, per * HALF, LANES), jnp.float32),
            jax.ShapeDtypeStruct((plan.home_slots + 8, CORES * plan.members * PARTS), jnp.float32),
        ),
        in_specs=[anywhere] * 5,
        out_specs=(in_vmem, in_vmem),
        scratch_shapes=[
            pltpu.SMEM((2, plan.pair_count), jnp.int32),
            pltpu.VMEM((2 * count, row_count), jnp.int32),
            pltpu.VMEM((tiles, LANES), jnp.bfloat16),
            pltpu.VMEM((tiles, LANES), jnp.bfloat16),
            pltpu.VMEM((1, plan.pair_count), jnp.int32),
            pltpu.VMEM((row_count, LANES), jnp.bfloat16),
            pltpu.VMEM((row_count, LANES), jnp.bfloat16),
            pltpu.VMEM((groups, GROUP * BINS, 2 * GROUP * BINS), jnp.float32),
            pltpu.SemaphoreType.DMA,
            pltpu.SemaphoreType.DMA((4,)),
        ],
        compiler_params=pltpu.CompilerParams(vmem_limit_bytes=SUMS_VMEM),
    )(*(pltpu.with_memory_space_constraint(operand, pltpu.HBM) for operand in operands))


def pair_gains(sums):
    upper = lax.broadcasted_iota(jnp.int32, sums.shape, 1) >= LANES // 2

    def margins(cum):
        end = jnp.where(upper, cum[:, 3 * BINS - 1 : 3 * BINS], cum[:, BINS - 1 : BINS])
        last = cum[HALF - 1 :]
        return cum, end, jnp.where(upper[:1], last, pltpu.roll(last, LANES // 2, 1)), last[:, 3 * BINS - 1 : 3 * BINS]

    grad_cum, grad_end, grad_col, grad_all = margins(sums)
    hess_cum, hess_end, hess_col, hess_all = margins(pltpu.roll(sums, LANES - BINS, 1))
    result = -(grad_all * grad_all) / (hess_all + LAMBDA_REG)
    for grad_part, hess_part in (
        (grad_cum, hess_cum),
        (grad_end - grad_cum, hess_end - hess_cum),
        (grad_col - grad_cum, hess_col - hess_cum),
        (grad_all - grad_end - grad_col + grad_cum, hess_all - hess_end - hess_col + hess_cum),
    ):
        result = result + grad_part * grad_part / (hess_part + LAMBDA_REG)
    return result


def gains_kernel(plan, start, count, per, parts_ref, out_ref, gains):
    share = BINS // plan.row_count
    lines = plan.row_count // 2
    total = parts_ref[0]
    for part in range(1, plan.row_count):
        total = total + parts_ref[part]
    place = per * seat(lax.axis_index("row"), plan.head)
    first_pair = lax.axis_index("feat") // CORES * plan.chip_pairs + start + place
    line = lax.broadcasted_iota(jnp.int32, (1, LANES), 1)
    wide = lax.broadcasted_iota(jnp.int32, (lines, LANES), 1)
    best = jnp.zeros((1, LANES), jnp.float32)
    cuts = []
    for pair in range(per):
        result = pair_gains(total[pair * HALF : (pair + 1) * HALF])
        gains[pair] = result
        peak = jnp.max(result, axis=0, keepdims=True)
        top = jnp.max(jnp.where(line % (2 * BINS) < BINS, peak, -jnp.inf), axis=1, keepdims=True)
        best = jnp.where((line == first_pair + pair) & (place + pair < count), top, best)
        halves = []
        for half in range(2):
            laid = None
            for step in range(share):
                rows = gains[pair, pl.ds(step, lines, stride=share), :] if share > 1 else result
                moved = (step - 2 * half) * BINS % LANES
                if moved:
                    rows = pltpu.roll(rows, moved, 1)
                laid = rows if laid is None else jnp.where(wide >= step * BINS, rows, laid)
            halves.append(laid)
        cuts.append(halves)
    spot = lax.broadcasted_iota(jnp.int32, (PARTS, LANES), 0)
    messages = []
    for row in range(plan.row_count):
        message = jnp.broadcast_to(best, (PARTS, LANES))
        for pair in range(per):
            at = row % lines
            message = jnp.where(spot == pair, cuts[pair][row // lines][at : at + 1], message)
        messages.append(message)
    for place, member in enumerate(plan.order):
        out_ref[place] = messages[member // plan.chips]


def table_kernel(route_ref, near_ref, far_ref, table_hbm, best_hbm, table, best, sems):
    ways = route_ref[...].astype(jnp.bfloat16)
    rest = jnp.concatenate([near_ref[...], far_ref[...]], axis=0)
    placed = jnp.zeros(route_ref.shape[:1] + rest.shape[1:], jnp.float32)
    for _ in range(3):
        part = rest.astype(jnp.bfloat16)
        rest = rest - part.astype(jnp.float32)
        placed = placed + jnp.dot(ways, part, preferred_element_type=jnp.float32)
    home_slots, width = table.shape
    table[...] = placed[:home_slots, :width]
    best[...] = placed[home_slots : home_slots + 1, : best.shape[1]]
    copies = (
        pltpu.make_async_copy(table, table_hbm, sems.at[0]),
        pltpu.make_async_copy(best, best_hbm, sems.at[1]),
    )
    for copy in copies:
        copy.start()
    for copy in copies:
        copy.wait()


def core_part(plan, core, *arguments):
    row_groups = [plan.rows]
    member_groups = [[member * CORES + side for member in plan.order] for side in range(CORES)]
    partial, ways = cut_sums(plan, core, *arguments)
    parts = lax.all_to_all(partial, "row", split_axis=0, concat_axis=0, tiled=True, axis_index_groups=row_groups)
    start, count, per = plan.start[core], plan.count[core], plan.per[core]
    in_vmem = pl.BlockSpec(memory_space=pltpu.VMEM)
    outgoing = pl.pallas_call(
        functools.partial(gains_kernel, plan, start, count, per),
        out_shape=jax.ShapeDtypeStruct((plan.members, PARTS, LANES), jnp.float32),
        in_specs=[in_vmem],
        out_specs=in_vmem,
        scratch_shapes=[pltpu.VMEM((per, HALF, LANES), jnp.float32)],
        compiler_params=pltpu.CompilerParams(vmem_limit_bytes=SMALL_VMEM),
    )(parts)
    near = lax.all_to_all(
        outgoing, ("row", "feat"), split_axis=0, concat_axis=0, tiled=True, axis_index_groups=member_groups
    )
    return near.reshape(plan.members * PARTS, LANES), ways


def shards(*arguments):
    feat_count = lax.axis_size("feat")
    plan = Plan(lax.axis_size("row"), feat_count, arguments[-1].shape[0])
    branches = [functools.partial(core_part, plan, core) for core in range(CORES)]
    near, ways = lax.cond(lax.axis_index("feat") % CORES == 0, *branches, *arguments)
    swap = [(feat, feat // CORES * CORES + (feat + 1) % CORES) for feat in range(feat_count)]
    far = lax.ppermute(near, "feat", swap)
    width = BINS // plan.row_count * BINS
    anywhere = pl.BlockSpec(memory_space=pl.ANY)
    cut_table, best = pl.pallas_call(
        table_kernel,
        out_shape=(
            jax.ShapeDtypeStruct((plan.home_slots, width), jnp.float32),
            jax.ShapeDtypeStruct((1, plan.pair_count), jnp.float32),
        ),
        in_specs=[pl.BlockSpec(memory_space=pltpu.VMEM)] * 3,
        out_specs=(anywhere, anywhere),
        scratch_shapes=[
            pltpu.VMEM((plan.home_slots, width), jnp.float32),
            pltpu.VMEM((1, plan.pair_count), jnp.float32),
            pltpu.SemaphoreType.DMA((2,)),
        ],
        compiler_params=pltpu.CompilerParams(vmem_limit_bytes=SMALL_VMEM),
    )(ways, near, far)
    return (cut_table, best.reshape(plan.pair_count))


def solution(mesh):
    in_specs = (P(None, "row"), P("row"), P("row"), P(), P())
    out_specs = (P("feat", "row"), P())
    return jax.shard_map(shards, mesh=mesh, in_specs=in_specs, out_specs=out_specs, check_vma=False)
```

```python
import functools

import jax
import jax.numpy as jnp
from jax import lax
from jax.experimental import pallas as pl
from jax.experimental.pallas import tpu as pltpu
from jax.sharding import PartitionSpec as P

BINS = 32
LAMBDA_REG = 1.0
LANES = 128
CORES = 2
GROUP = 4
HALF = BINS // 2
PARTS = 4
CHUNK = 2048
HEAD = 5
LATE_HEAD = 5
SUMS_VMEM = 48 * 2**20
SMALL_VMEM = 4 * 2**20


class Plan:
    def __init__(self, row_count, feat_count, pair_count):
        self.row_count = row_count
        self.pair_count = pair_count
        self.chips = feat_count // CORES
        self.chip_pairs = pair_count // self.chips
        self.home_slots = 2 * pair_count // feat_count
        light = self.chip_pairs // GROUP // 4 * GROUP
        self.start = (0, light)
        self.count = (light, self.chip_pairs - light)
        self.per = tuple(-(-count // row_count) for count in self.count)
        self.head = HEAD * row_count // 8
        self.rows = [self.head] + [row for row in range(row_count) if row != self.head]
        self.members = row_count * self.chips
        self.late_head = LATE_HEAD * row_count // 8 * self.chips + self.chips - 1
        self.order = [self.late_head] + [member for member in range(self.members) if member != self.late_head]


def seat(member, head):
    return jnp.where(member == head, 0, jnp.where(member < head, member + 1, member))


def sitter(place, head):
    return jnp.where(place == 0, head, jnp.where(place <= head, place - 1, place))


def route_tables(plan):
    shape = (plan.pair_count, CORES * plan.members * PARTS)
    spot = lax.broadcasted_iota(jnp.int32, shape, 1)
    part, seated, other = spot % PARTS, spot // PARTS % plan.members, spot // (PARTS * plan.members)
    device = sitter(seated, plan.late_head)
    light = (lax.axis_index("feat") + other) % CORES == 0
    per, start, count = (jnp.where(light, values[0], values[1]) for values in (plan.per, plan.start, plan.count))
    place = seat(device // plan.chips, plan.head) * per + part
    pair = device % plan.chips * plan.chip_pairs + start + place
    held = (part < per) & (place < count)
    holders = held & (pair == lax.broadcasted_iota(jnp.int32, shape, 0))
    square = (plan.pair_count, plan.pair_count)
    earlier = lax.broadcasted_iota(jnp.int32, square, 0) < lax.broadcasted_iota(jnp.int32, square, 1)
    return holders.astype(jnp.float32), earlier.astype(jnp.float32)


def route(mine, holders, earlier, home_slots, shape):
    owned = jnp.broadcast_to(mine.astype(jnp.float32), (8, mine.shape[1]))
    rank = jnp.dot(owned, earlier, preferred_element_type=jnp.float32)
    upper = lax.broadcasted_iota(jnp.int32, owned.shape, 0) == 0
    spread = jnp.dot(jnp.where(upper, owned, rank), holders, preferred_element_type=jnp.float32)
    slot = lax.broadcasted_iota(jnp.int32, shape, 0)
    taken = jnp.where(spread[1:2].astype(jnp.int32) == slot, spread[0:1], 0.0)
    best_row = jnp.where(lax.broadcasted_iota(jnp.int32, shape, 1) % PARTS == PARTS - 1, 1.0, 0.0)
    return jnp.where(slot < home_slots, taken, best_row)


def cut_sums_kernel(
    plan, start, count, per, pairs_hbm, codes_hbm, grad_hbm, hess_hbm, owners_hbm, out_ref, route_ref,
    pairs, codes, grad, hess, owners, grad_tall, hess_tall, sums, code_sem, small_sems,
):
    groups = count // GROUP
    row_count = codes.shape[1]
    row_messages = out_ref.shape[0]
    feat_index = lax.axis_index("feat")
    first_pair = feat_index // CORES * plan.chip_pairs + start
    pairs_copy = pltpu.make_async_copy(pairs_hbm, pairs, small_sems.at[0])
    grad_copy = pltpu.make_async_copy(grad_hbm, grad, small_sems.at[1])
    hess_copy = pltpu.make_async_copy(hess_hbm, hess, small_sems.at[2])
    owners_copy = pltpu.make_async_copy(owners_hbm, owners, small_sems.at[3])
    pairs_copy.start()
    grad_copy.start()
    hess_copy.start()
    owners_copy.start()
    holders, earlier = route_tables(plan)
    pairs_copy.wait()

    for line in range(2 * count):
        feature = pairs[line % 2, first_pair + line // 2]
        pltpu.make_async_copy(codes_hbm.at[pl.ds(feature, 1)], codes.at[pl.ds(line, 1)], code_sem).start()
    levels = lax.broadcasted_iota(jnp.int32, (HALF, 1), 0).astype(jnp.float32)
    level_parts = (levels.astype(jnp.bfloat16), (levels + HALF).astype(jnp.bfloat16))
    grad_copy.wait()
    hess_copy.wait()
    owners_copy.wait()
    route_ref[...] = route(owners[...] == feat_index, holders, earlier, plan.home_slots, route_ref.shape)
    for flat, tall in ((grad, grad_tall), (hess, hess_tall)):
        values = flat[...].astype(jnp.float32)
        for tile in range(row_count // LANES):
            square = jnp.broadcast_to(values[tile : tile + 1], (LANES, LANES)).astype(jnp.bfloat16)
            tall[tile * LANES : (tile + 1) * LANES, :] = square.T
    zero = jnp.zeros((HALF, CHUNK), jnp.bfloat16)
    one = jnp.ones((HALF, CHUNK), jnp.bfloat16)

    def below(line, span):
        values = codes[line : line + 1, span].astype(jnp.float32)
        values = jnp.broadcast_to(values, (HALF, CHUNK)).astype(jnp.bfloat16)
        return [jnp.where(values <= level, one, zero) for level in level_parts]

    pltpu.make_async_copy(codes_hbm.at[pl.ds(0, 2 * count)], codes, code_sem).wait()
    for group in range(groups):
        total = None
        for begin in range(0, row_count, CHUNK):
            span = slice(begin, begin + CHUNK)
            first_rows, second_rows = [], []
            for pair in range(GROUP):
                line = 2 * (GROUP * group + pair)
                first_rows += below(line, span)
                second_rows += below(line + 1, span)
            first = jnp.concatenate(first_rows, axis=0)
            second = jnp.concatenate(second_rows, axis=0).T
            weighted = jnp.concatenate([second * grad_tall[span, :], second * hess_tall[span, :]], axis=1)
            product = jnp.dot(first, weighted, preferred_element_type=jnp.float32)
            total = product if total is None else total + product
        sums[group] = total
    lane = lax.broadcasted_iota(jnp.int32, (HALF, LANES), 1)
    for place in range(row_messages * per):
        message, at = place // per, place % per * HALF
        if place >= count:
            out_ref[message, at : at + HALF] = jnp.zeros((HALF, LANES), jnp.float32)
            continue
        group, pair = place // GROUP, place % GROUP
        block = None
        for quarter in range(4):
            top, left = pair * BINS + quarter // 2 * HALF, quarter % 2 * LANES
            piece = sums[group, top : top + HALF, left : left + LANES]
            moved = (quarter - pair) * BINS % LANES
            if moved:
                piece = pltpu.roll(piece, moved, 1)
            block = piece if block is None else jnp.where(lane >= quarter * BINS, piece, block)
        out_ref[message, at : at + HALF] = block


def cut_sums(plan, core, bin_codes, gradients, hessians, pair_list, owners):
    row_count = bin_codes.shape[1]
    start, count, per = plan.start[core], plan.count[core], plan.per[core]
    groups = count // GROUP
    tiles = row_count // LANES
    anywhere = pl.BlockSpec(memory_space=pl.ANY)
    in_vmem = pl.BlockSpec(memory_space=pltpu.VMEM)
    flat = (gradients.reshape(tiles, LANES), hessians.reshape(tiles, LANES), owners.reshape(1, plan.pair_count))
    operands = (pair_list.T, bin_codes) + flat
    return pl.pallas_call(
        functools.partial(cut_sums_kernel, plan, start, count, per),
        out_shape=(
            jax.ShapeDtypeStruct((plan.row_count, per * HALF, LANES), jnp.float32),
            jax.ShapeDtypeStruct((plan.home_slots + 8, CORES * plan.members * PARTS), jnp.float32),
        ),
        in_specs=[anywhere] * 5,
        out_specs=(in_vmem, in_vmem),
        scratch_shapes=[
            pltpu.SMEM((2, plan.pair_count), jnp.int32),
            pltpu.VMEM((2 * count, row_count), jnp.int32),
            pltpu.VMEM((tiles, LANES), jnp.bfloat16),
            pltpu.VMEM((tiles, LANES), jnp.bfloat16),
            pltpu.VMEM((1, plan.pair_count), jnp.int32),
            pltpu.VMEM((row_count, LANES), jnp.bfloat16),
            pltpu.VMEM((row_count, LANES), jnp.bfloat16),
            pltpu.VMEM((groups, GROUP * BINS, 2 * GROUP * BINS), jnp.float32),
            pltpu.SemaphoreType.DMA,
            pltpu.SemaphoreType.DMA((4,)),
        ],
        compiler_params=pltpu.CompilerParams(vmem_limit_bytes=SUMS_VMEM),
    )(*(pltpu.with_memory_space_constraint(operand, pltpu.HBM) for operand in operands))


def pair_gains(sums):
    upper = lax.broadcasted_iota(jnp.int32, sums.shape, 1) >= LANES // 2

    def margins(cum):
        end = jnp.where(upper, cum[:, 3 * BINS - 1 : 3 * BINS], cum[:, BINS - 1 : BINS])
        last = cum[HALF - 1 :]
        return cum, end, jnp.where(upper[:1], last, pltpu.roll(last, LANES // 2, 1)), last[:, 3 * BINS - 1 : 3 * BINS]

    grad_cum, grad_end, grad_col, grad_all = margins(sums)
    hess_cum, hess_end, hess_col, hess_all = margins(pltpu.roll(sums, LANES - BINS, 1))
    result = -(grad_all * grad_all) / (hess_all + LAMBDA_REG)
    for grad_part, hess_part in (
        (grad_cum, hess_cum),
        (grad_end - grad_cum, hess_end - hess_cum),
        (grad_col - grad_cum, hess_col - hess_cum),
        (grad_all - grad_end - grad_col + grad_cum, hess_all - hess_end - hess_col + hess_cum),
    ):
        result = result + grad_part * grad_part / (hess_part + LAMBDA_REG)
    return result


def gains_kernel(plan, start, count, per, parts_ref, out_ref, gains):
    share = BINS // plan.row_count
    lines = plan.row_count // 2
    total = parts_ref[0]
    for part in range(1, plan.row_count):
        total = total + parts_ref[part]
    place = per * seat(lax.axis_index("row"), plan.head)
    first_pair = lax.axis_index("feat") // CORES * plan.chip_pairs + start + place
    line = lax.broadcasted_iota(jnp.int32, (1, LANES), 1)
    wide = lax.broadcasted_iota(jnp.int32, (lines, LANES), 1)
    best = jnp.zeros((1, LANES), jnp.float32)
    cuts = []
    for pair in range(per):
        result = pair_gains(total[pair * HALF : (pair + 1) * HALF])
        gains[pair] = result
        peak = jnp.max(result, axis=0, keepdims=True)
        top = jnp.max(jnp.where(line % (2 * BINS) < BINS, peak, -jnp.inf), axis=1, keepdims=True)
        best = jnp.where((line == first_pair + pair) & (place + pair < count), top, best)
        halves = []
        for half in range(2):
            laid = None
            for step in range(share):
                rows = gains[pair, pl.ds(step, lines, stride=share), :] if share > 1 else result
                moved = (step - 2 * half) * BINS % LANES
                if moved:
                    rows = pltpu.roll(rows, moved, 1)
                laid = rows if laid is None else jnp.where(wide >= step * BINS, rows, laid)
            halves.append(laid)
        cuts.append(halves)
    spot = lax.broadcasted_iota(jnp.int32, (PARTS, LANES), 0)
    messages = []
    for row in range(plan.row_count):
        message = jnp.broadcast_to(best, (PARTS, LANES))
        for pair in range(per):
            at = row % lines
            message = jnp.where(spot == pair, cuts[pair][row // lines][at : at + 1], message)
        messages.append(message)
    for place, member in enumerate(plan.order):
        out_ref[place] = messages[member // plan.chips]


def table_kernel(route_ref, near_ref, far_ref, table_hbm, best_hbm, table, best, sems):
    ways = route_ref[...].astype(jnp.bfloat16)
    rest = jnp.concatenate([near_ref[...], far_ref[...]], axis=0)
    placed = jnp.zeros(route_ref.shape[:1] + rest.shape[1:], jnp.float32)
    for _ in range(3):
        part = rest.astype(jnp.bfloat16)
        rest = rest - part.astype(jnp.float32)
        placed = placed + jnp.dot(ways, part, preferred_element_type=jnp.float32)
    home_slots, width = table.shape
    table[...] = placed[:home_slots, :width]
    best[...] = placed[home_slots : home_slots + 1, : best.shape[1]]
    copies = (
        pltpu.make_async_copy(table, table_hbm, sems.at[0]),
        pltpu.make_async_copy(best, best_hbm, sems.at[1]),
    )
    for copy in copies:
        copy.start()
    for copy in copies:
        copy.wait()


def core_part(plan, core, *arguments):
    row_groups = [plan.rows]
    member_groups = [[member * CORES + side for member in plan.order] for side in range(CORES)]
    partial, ways = cut_sums(plan, core, *arguments)
    parts = lax.all_to_all(partial, "row", split_axis=0, concat_axis=0, tiled=True, axis_index_groups=row_groups)
    start, count, per = plan.start[core], plan.count[core], plan.per[core]
    in_vmem = pl.BlockSpec(memory_space=pltpu.VMEM)
    outgoing = pl.pallas_call(
        functools.partial(gains_kernel, plan, start, count, per),
        out_shape=jax.ShapeDtypeStruct((plan.members, PARTS, LANES), jnp.float32),
        in_specs=[in_vmem],
        out_specs=in_vmem,
        scratch_shapes=[pltpu.VMEM((per, HALF, LANES), jnp.float32)],
        compiler_params=pltpu.CompilerParams(vmem_limit_bytes=SMALL_VMEM),
    )(parts)
    near = lax.all_to_all(
        outgoing, ("row", "feat"), split_axis=0, concat_axis=0, tiled=True, axis_index_groups=member_groups
    )
    return near.reshape(plan.members * PARTS, LANES), ways


def shards(*arguments):
    feat_count = lax.axis_size("feat")
    plan = Plan(lax.axis_size("row"), feat_count, arguments[-1].shape[0])
    branches = [functools.partial(core_part, plan, core) for core in range(CORES)]
    near, ways = lax.cond(lax.axis_index("feat") % CORES == 0, *branches, *arguments)
    swap = [(feat, feat // CORES * CORES + (feat + 1) % CORES) for feat in range(feat_count)]
    far = lax.ppermute(near, "feat", swap)
    width = BINS // plan.row_count * BINS
    anywhere = pl.BlockSpec(memory_space=pl.ANY)
    cut_table, best = pl.pallas_call(
        table_kernel,
        out_shape=(
            jax.ShapeDtypeStruct((plan.home_slots, width), jnp.float32),
            jax.ShapeDtypeStruct((1, plan.pair_count), jnp.float32),
        ),
        in_specs=[pl.BlockSpec(memory_space=pltpu.VMEM)] * 3,
        out_specs=(anywhere, anywhere),
        scratch_shapes=[
            pltpu.VMEM((plan.home_slots, width), jnp.float32),
            pltpu.VMEM((1, plan.pair_count), jnp.float32),
            pltpu.SemaphoreType.DMA((2,)),
        ],
        compiler_params=pltpu.CompilerParams(vmem_limit_bytes=SMALL_VMEM),
    )(ways, near, far)
    return (cut_table, best.reshape(plan.pair_count))


def solution(mesh):
    in_specs = (P(None, "row"), P("row"), P("row"), P(), P())
    out_specs = (P("feat", "row"), P())
    return jax.shard_map(shards, mesh=mesh, in_specs=in_specs, out_specs=out_specs, check_vma=False)
```

```python
import functools

import jax
import jax.numpy as jnp
from jax import lax
from jax.experimental import pallas as pl
from jax.experimental.pallas import tpu as pltpu
from jax.sharding import PartitionSpec as P

BINS = 32
LAMBDA_REG = 1.0
LANES = 128
CORES = 2
GROUP = 4
HALF = BINS // 2
PARTS = 4
CHUNK = 2048
HEAD = 5
LATE_HEAD = 5
ROW_ORDERS = {8: [5, 1, 0, 2, 3, 7, 4, 6]}
MEMBER_ORDERS = {16: [11, 10, 12, 5, 9, 0, 6, 3, 15, 8, 1, 14, 7, 2, 13, 4]}
SUMS_VMEM = 48 * 2**20
SMALL_VMEM = 4 * 2**20


class Plan:
    def __init__(self, row_count, feat_count, pair_count):
        self.row_count = row_count
        self.pair_count = pair_count
        self.chips = feat_count // CORES
        self.chip_pairs = pair_count // self.chips
        self.home_slots = 2 * pair_count // feat_count
        light = self.chip_pairs // GROUP // 4 * GROUP
        self.start = (0, light)
        self.count = (light, self.chip_pairs - light)
        self.per = tuple(-(-count // row_count) for count in self.count)
        self.rows = group_order(row_count, HEAD * row_count // 8, ROW_ORDERS)
        self.members = row_count * self.chips
        late_head = LATE_HEAD * row_count // 8 * self.chips + self.chips - 1
        self.order = group_order(self.members, late_head, MEMBER_ORDERS)


def group_order(size, head, orders):
    return orders.get(size, [head] + [member for member in range(size) if member != head])


def seat(member, order):
    head = order[0]
    if order[1:] == sorted(order[1:]):
        return jnp.where(member == head, 0, jnp.where(member < head, member + 1, member))
    place = jnp.zeros_like(member)
    for at, who in enumerate(order):
        place = jnp.where(member == who, at, place)
    return place


def sitter(place, order):
    head = order[0]
    if order[1:] == sorted(order[1:]):
        return jnp.where(place == 0, head, jnp.where(place <= head, place - 1, place))
    member = jnp.zeros_like(place)
    for at, who in enumerate(order):
        member = jnp.where(place == at, who, member)
    return member


def route_tables(plan):
    shape = (plan.pair_count, CORES * plan.members * PARTS)
    spot = lax.broadcasted_iota(jnp.int32, shape, 1)
    part, seated, other = spot % PARTS, spot // PARTS % plan.members, spot // (PARTS * plan.members)
    device = sitter(seated, plan.order)
    light = (lax.axis_index("feat") + other) % CORES == 0
    per, start, count = (jnp.where(light, values[0], values[1]) for values in (plan.per, plan.start, plan.count))
    place = seat(device // plan.chips, plan.rows) * per + part
    pair = device % plan.chips * plan.chip_pairs + start + place
    held = (part < per) & (place < count)
    holders = held & (pair == lax.broadcasted_iota(jnp.int32, shape, 0))
    square = (plan.pair_count, plan.pair_count)
    earlier = lax.broadcasted_iota(jnp.int32, square, 0) < lax.broadcasted_iota(jnp.int32, square, 1)
    return holders.astype(jnp.float32), earlier.astype(jnp.float32)


def route(mine, holders, earlier, home_slots, shape):
    owned = jnp.broadcast_to(mine.astype(jnp.float32), (8, mine.shape[1]))
    rank = jnp.dot(owned, earlier, preferred_element_type=jnp.float32)
    upper = lax.broadcasted_iota(jnp.int32, owned.shape, 0) == 0
    spread = jnp.dot(jnp.where(upper, owned, rank), holders, preferred_element_type=jnp.float32)
    slot = lax.broadcasted_iota(jnp.int32, shape, 0)
    taken = jnp.where(spread[1:2].astype(jnp.int32) == slot, spread[0:1], 0.0)
    best_row = jnp.where(lax.broadcasted_iota(jnp.int32, shape, 1) % PARTS == PARTS - 1, 1.0, 0.0)
    return jnp.where(slot < home_slots, taken, best_row)


def cut_sums_kernel(
    plan, start, count, per, pairs_hbm, codes_hbm, grad_hbm, hess_hbm, owners_hbm, out_ref, route_ref,
    pairs, codes, grad, hess, owners, grad_tall, hess_tall, sums, code_sem, small_sems,
):
    groups = count // GROUP
    row_count = codes.shape[1]
    row_messages = out_ref.shape[0]
    feat_index = lax.axis_index("feat")
    first_pair = feat_index // CORES * plan.chip_pairs + start
    pairs_copy = pltpu.make_async_copy(pairs_hbm, pairs, small_sems.at[0])
    grad_copy = pltpu.make_async_copy(grad_hbm, grad, small_sems.at[1])
    hess_copy = pltpu.make_async_copy(hess_hbm, hess, small_sems.at[2])
    owners_copy = pltpu.make_async_copy(owners_hbm, owners, small_sems.at[3])
    pairs_copy.start()
    grad_copy.start()
    hess_copy.start()
    owners_copy.start()
    holders, earlier = route_tables(plan)
    pairs_copy.wait()

    for line in range(2 * count):
        feature = pairs[line % 2, first_pair + line // 2]
        pltpu.make_async_copy(codes_hbm.at[pl.ds(feature, 1)], codes.at[pl.ds(line, 1)], code_sem).start()
    levels = lax.broadcasted_iota(jnp.int32, (HALF, 1), 0).astype(jnp.float32)
    level_parts = (levels.astype(jnp.bfloat16), (levels + HALF).astype(jnp.bfloat16))
    grad_copy.wait()
    hess_copy.wait()
    owners_copy.wait()
    route_ref[...] = route(owners[...] == feat_index, holders, earlier, plan.home_slots, route_ref.shape)
    for flat, tall in ((grad, grad_tall), (hess, hess_tall)):
        values = flat[...].astype(jnp.float32)
        for tile in range(row_count // LANES):
            square = jnp.broadcast_to(values[tile : tile + 1], (LANES, LANES)).astype(jnp.bfloat16)
            tall[tile * LANES : (tile + 1) * LANES, :] = square.T
    zero = jnp.zeros((HALF, CHUNK), jnp.bfloat16)
    one = jnp.ones((HALF, CHUNK), jnp.bfloat16)

    def below(line, span):
        values = codes[line : line + 1, span].astype(jnp.float32)
        values = jnp.broadcast_to(values, (HALF, CHUNK)).astype(jnp.bfloat16)
        return [jnp.where(values <= level, one, zero) for level in level_parts]

    pltpu.make_async_copy(codes_hbm.at[pl.ds(0, 2 * count)], codes, code_sem).wait()
    for group in range(groups):
        total = None
        for begin in range(0, row_count, CHUNK):
            span = slice(begin, begin + CHUNK)
            first_rows, second_rows = [], []
            for pair in range(GROUP):
                line = 2 * (GROUP * group + pair)
                first_rows += below(line, span)
                second_rows += below(line + 1, span)
            first = jnp.concatenate(first_rows, axis=0)
            second = jnp.concatenate(second_rows, axis=0).T
            weighted = jnp.concatenate([second * grad_tall[span, :], second * hess_tall[span, :]], axis=1)
            product = jnp.dot(first, weighted, preferred_element_type=jnp.float32)
            total = product if total is None else total + product
        sums[group] = total
    lane = lax.broadcasted_iota(jnp.int32, (HALF, LANES), 1)
    for place in range(row_messages * per):
        message, at = place // per, place % per * HALF
        if place >= count:
            out_ref[message, at : at + HALF] = jnp.zeros((HALF, LANES), jnp.float32)
            continue
        group, pair = place // GROUP, place % GROUP
        block = None
        for quarter in range(4):
            top, left = pair * BINS + quarter // 2 * HALF, quarter % 2 * LANES
            piece = sums[group, top : top + HALF, left : left + LANES]
            moved = (quarter - pair) * BINS % LANES
            if moved:
                piece = pltpu.roll(piece, moved, 1)
            block = piece if block is None else jnp.where(lane >= quarter * BINS, piece, block)
        out_ref[message, at : at + HALF] = block


def cut_sums(plan, core, bin_codes, gradients, hessians, pair_list, owners):
    row_count = bin_codes.shape[1]
    start, count, per = plan.start[core], plan.count[core], plan.per[core]
    groups = count // GROUP
    tiles = row_count // LANES
    anywhere = pl.BlockSpec(memory_space=pl.ANY)
    in_vmem = pl.BlockSpec(memory_space=pltpu.VMEM)
    flat = (gradients.reshape(tiles, LANES), hessians.reshape(tiles, LANES), owners.reshape(1, plan.pair_count))
    operands = (pair_list.T, bin_codes) + flat
    return pl.pallas_call(
        functools.partial(cut_sums_kernel, plan, start, count, per),
        out_shape=(
            jax.ShapeDtypeStruct((plan.row_count, per * HALF, LANES), jnp.float32),
            jax.ShapeDtypeStruct((plan.home_slots + 8, CORES * plan.members * PARTS), jnp.float32),
        ),
        in_specs=[anywhere] * 5,
        out_specs=(in_vmem, in_vmem),
        scratch_shapes=[
            pltpu.SMEM((2, plan.pair_count), jnp.int32),
            pltpu.VMEM((2 * count, row_count), jnp.int32),
            pltpu.VMEM((tiles, LANES), jnp.bfloat16),
            pltpu.VMEM((tiles, LANES), jnp.bfloat16),
            pltpu.VMEM((1, plan.pair_count), jnp.int32),
            pltpu.VMEM((row_count, LANES), jnp.bfloat16),
            pltpu.VMEM((row_count, LANES), jnp.bfloat16),
            pltpu.VMEM((groups, GROUP * BINS, 2 * GROUP * BINS), jnp.float32),
            pltpu.SemaphoreType.DMA,
            pltpu.SemaphoreType.DMA((4,)),
        ],
        compiler_params=pltpu.CompilerParams(vmem_limit_bytes=SUMS_VMEM),
    )(*(pltpu.with_memory_space_constraint(operand, pltpu.HBM) for operand in operands))


def pair_gains(sums):
    upper = lax.broadcasted_iota(jnp.int32, sums.shape, 1) >= LANES // 2

    def margins(cum):
        end = jnp.where(upper, cum[:, 3 * BINS - 1 : 3 * BINS], cum[:, BINS - 1 : BINS])
        last = cum[HALF - 1 :]
        return cum, end, jnp.where(upper[:1], last, pltpu.roll(last, LANES // 2, 1)), last[:, 3 * BINS - 1 : 3 * BINS]

    grad_cum, grad_end, grad_col, grad_all = margins(sums)
    hess_cum, hess_end, hess_col, hess_all = margins(pltpu.roll(sums, LANES - BINS, 1))
    result = -(grad_all * grad_all) / (hess_all + LAMBDA_REG)
    for grad_part, hess_part in (
        (grad_cum, hess_cum),
        (grad_end - grad_cum, hess_end - hess_cum),
        (grad_col - grad_cum, hess_col - hess_cum),
        (grad_all - grad_end - grad_col + grad_cum, hess_all - hess_end - hess_col + hess_cum),
    ):
        result = result + grad_part * grad_part / (hess_part + LAMBDA_REG)
    return result


def gains_kernel(plan, start, count, per, parts_ref, out_ref, gains):
    share = BINS // plan.row_count
    lines = plan.row_count // 2
    total = parts_ref[0]
    for part in range(1, plan.row_count):
        total = total + parts_ref[part]
    place = per * seat(lax.axis_index("row"), plan.rows)
    first_pair = lax.axis_index("feat") // CORES * plan.chip_pairs + start + place
    line = lax.broadcasted_iota(jnp.int32, (1, LANES), 1)
    wide = lax.broadcasted_iota(jnp.int32, (lines, LANES), 1)
    best = jnp.zeros((1, LANES), jnp.float32)
    cuts = []
    for pair in range(per):
        result = pair_gains(total[pair * HALF : (pair + 1) * HALF])
        gains[pair] = result
        peak = jnp.max(result, axis=0, keepdims=True)
        top = jnp.max(jnp.where(line % (2 * BINS) < BINS, peak, -jnp.inf), axis=1, keepdims=True)
        best = jnp.where((line == first_pair + pair) & (place + pair < count), top, best)
        halves = []
        for half in range(2):
            laid = None
            for step in range(share):
                rows = gains[pair, pl.ds(step, lines, stride=share), :] if share > 1 else result
                moved = (step - 2 * half) * BINS % LANES
                if moved:
                    rows = pltpu.roll(rows, moved, 1)
                laid = rows if laid is None else jnp.where(wide >= step * BINS, rows, laid)
            halves.append(laid)
        cuts.append(halves)
    spot = lax.broadcasted_iota(jnp.int32, (PARTS, LANES), 0)
    messages = []
    for row in range(plan.row_count):
        message = jnp.broadcast_to(best, (PARTS, LANES))
        for pair in range(per):
            at = row % lines
            message = jnp.where(spot == pair, cuts[pair][row // lines][at : at + 1], message)
        messages.append(message)
    for place, member in enumerate(plan.order):
        out_ref[place] = messages[member // plan.chips]


def table_kernel(route_ref, near_ref, far_ref, table, best):
    ways = route_ref[...].astype(jnp.bfloat16)
    rest = jnp.concatenate([near_ref[...], far_ref[...]], axis=0)
    placed = jnp.zeros(route_ref.shape[:1] + rest.shape[1:], jnp.float32)
    for _ in range(3):
        part = rest.astype(jnp.bfloat16)
        rest = rest - part.astype(jnp.float32)
        placed = placed + jnp.dot(ways, part, preferred_element_type=jnp.float32)
    home_slots, width = table.shape
    table[...] = placed[:home_slots, :width]
    best[...] = placed[home_slots : home_slots + 1, : best.shape[1]]


def core_part(plan, core, *arguments):
    row_groups = [plan.rows]
    member_groups = [[member * CORES + side for member in plan.order] for side in range(CORES)]
    partial, ways = cut_sums(plan, core, *arguments)
    parts = lax.all_to_all(partial, "row", split_axis=0, concat_axis=0, tiled=True, axis_index_groups=row_groups)
    start, count, per = plan.start[core], plan.count[core], plan.per[core]
    in_vmem = pl.BlockSpec(memory_space=pltpu.VMEM)
    outgoing = pl.pallas_call(
        functools.partial(gains_kernel, plan, start, count, per),
        out_shape=jax.ShapeDtypeStruct((plan.members, PARTS, LANES), jnp.float32),
        in_specs=[in_vmem],
        out_specs=in_vmem,
        scratch_shapes=[pltpu.VMEM((per, HALF, LANES), jnp.float32)],
        compiler_params=pltpu.CompilerParams(vmem_limit_bytes=SMALL_VMEM),
    )(parts)
    near = lax.all_to_all(
        outgoing, ("row", "feat"), split_axis=0, concat_axis=0, tiled=True, axis_index_groups=member_groups
    )
    return near.reshape(plan.members * PARTS, LANES), ways


def shards(*arguments):
    feat_count = lax.axis_size("feat")
    plan = Plan(lax.axis_size("row"), feat_count, arguments[-1].shape[0])
    branches = [functools.partial(core_part, plan, core) for core in range(CORES)]
    near, ways = lax.cond(lax.axis_index("feat") % CORES == 0, *branches, *arguments)
    swap = [(feat, feat // CORES * CORES + (feat + 1) % CORES) for feat in range(feat_count)]
    far = lax.ppermute(near, "feat", swap)
    width = BINS // plan.row_count * BINS
    cut_table, best = pl.pallas_call(
        table_kernel,
        out_shape=(
            jax.ShapeDtypeStruct((plan.home_slots, width), jnp.float32),
            jax.ShapeDtypeStruct((1, plan.pair_count), jnp.float32),
        ),
        in_specs=[pl.BlockSpec(memory_space=pltpu.VMEM)] * 3,
        out_specs=[pl.BlockSpec(memory_space=pltpu.VMEM)] * 2,
        compiler_params=pltpu.CompilerParams(vmem_limit_bytes=SMALL_VMEM),
    )(ways, near, far)
    return (cut_table, best.reshape(plan.pair_count))


def solution(mesh):
    in_specs = (P(None, "row"), P("row"), P("row"), P(), P())
    out_specs = (P("feat", "row"), P())
    return jax.shard_map(shards, mesh=mesh, in_specs=in_specs, out_specs=out_specs, check_vma=False)
```

```python
import functools

import jax
import jax.numpy as jnp
from jax import lax
from jax.experimental import pallas as pl
from jax.experimental.pallas import tpu as pltpu
from jax.sharding import PartitionSpec as P

BINS = 32
LAMBDA_REG = 1.0
LANES = 128
CORES = 2
GROUP = 4
HALF = BINS // 2
PARTS = 4
CHUNK = 2048
HEAD = 5
LATE_HEAD = 5
ROW_ORDERS = {8: [5, 1, 0, 2, 3, 7, 4, 6]}
MEMBER_ORDERS = {16: [11, 10, 12, 5, 9, 0, 6, 3, 15, 8, 1, 14, 7, 2, 13, 4]}
SUMS_VMEM = 48 * 2**20
SMALL_VMEM = 4 * 2**20


class Plan:
    def __init__(self, row_count, feat_count, pair_count):
        self.row_count = row_count
        self.pair_count = pair_count
        self.chips = feat_count // CORES
        self.chip_pairs = pair_count // self.chips
        self.home_slots = 2 * pair_count // feat_count
        light = self.chip_pairs // GROUP // 4 * GROUP
        self.start = (0, light)
        self.count = (light, self.chip_pairs - light)
        self.per = tuple(-(-count // row_count) for count in self.count)
        self.rows = group_order(row_count, HEAD * row_count // 8, ROW_ORDERS)
        self.members = row_count * self.chips
        late_head = LATE_HEAD * row_count // 8 * self.chips + self.chips - 1
        self.order = group_order(self.members, late_head, MEMBER_ORDERS)


def group_order(size, head, orders):
    return orders.get(size, [head] + [member for member in range(size) if member != head])


def seat(member, order):
    head = order[0]
    if order[1:] == sorted(order[1:]):
        return jnp.where(member == head, 0, jnp.where(member < head, member + 1, member))
    place = jnp.zeros_like(member)
    for at, who in enumerate(order):
        place = jnp.where(member == who, at, place)
    return place


def sitter(place, order):
    head = order[0]
    if order[1:] == sorted(order[1:]):
        return jnp.where(place == 0, head, jnp.where(place <= head, place - 1, place))
    member = jnp.zeros_like(place)
    for at, who in enumerate(order):
        member = jnp.where(place == at, who, member)
    return member


def route_tables(plan):
    shape = (plan.pair_count, CORES * plan.members * PARTS)
    spot = lax.broadcasted_iota(jnp.int32, shape, 1)
    part, seated, other = spot % PARTS, spot // PARTS % plan.members, spot // (PARTS * plan.members)
    device = sitter(seated, plan.order)
    light = (lax.axis_index("feat") + other) % CORES == 0
    per, start, count = (jnp.where(light, values[0], values[1]) for values in (plan.per, plan.start, plan.count))
    place = seat(device // plan.chips, plan.rows) * per + part
    pair = device % plan.chips * plan.chip_pairs + start + place
    held = (part < per) & (place < count)
    holders = held & (pair == lax.broadcasted_iota(jnp.int32, shape, 0))
    square = (plan.pair_count, plan.pair_count)
    earlier = lax.broadcasted_iota(jnp.int32, square, 0) < lax.broadcasted_iota(jnp.int32, square, 1)
    return holders.astype(jnp.float32), earlier.astype(jnp.float32)


def route(mine, holders, earlier, home_slots, shape):
    owned = jnp.broadcast_to(mine.astype(jnp.float32), (8, mine.shape[1]))
    rank = jnp.dot(owned, earlier, preferred_element_type=jnp.float32)
    upper = lax.broadcasted_iota(jnp.int32, owned.shape, 0) == 0
    spread = jnp.dot(jnp.where(upper, owned, rank), holders, preferred_element_type=jnp.float32)
    slot = lax.broadcasted_iota(jnp.int32, shape, 0)
    taken = jnp.where(spread[1:2].astype(jnp.int32) == slot, spread[0:1], 0.0)
    best_row = jnp.where(lax.broadcasted_iota(jnp.int32, shape, 1) % PARTS == PARTS - 1, 1.0, 0.0)
    return jnp.where(slot < home_slots, taken, best_row)


def cut_sums_kernel(
    plan, start, count, per, pairs_hbm, codes_hbm, grad_hbm, hess_hbm, owners_hbm, out_ref, route_ref,
    pairs, codes, grad, hess, owners, grad_tall, hess_tall, sums, code_sem, small_sems,
):
    groups = count // GROUP
    row_count = codes.shape[1]
    row_messages = out_ref.shape[0]
    feat_index = lax.axis_index("feat")
    first_pair = feat_index // CORES * plan.chip_pairs + start
    pairs_copy = pltpu.make_async_copy(pairs_hbm, pairs, small_sems.at[0])
    grad_copy = pltpu.make_async_copy(grad_hbm, grad, small_sems.at[1])
    hess_copy = pltpu.make_async_copy(hess_hbm, hess, small_sems.at[2])
    owners_copy = pltpu.make_async_copy(owners_hbm, owners, small_sems.at[3])
    pairs_copy.start()
    grad_copy.start()
    hess_copy.start()
    owners_copy.start()
    holders, earlier = route_tables(plan)
    pairs_copy.wait()

    for line in range(2 * count):
        feature = pairs[line % 2, first_pair + line // 2]
        pltpu.make_async_copy(codes_hbm.at[pl.ds(feature, 1)], codes.at[pl.ds(line, 1)], code_sem).start()
    levels = lax.broadcasted_iota(jnp.int32, (HALF, 1), 0).astype(jnp.float32)
    level_parts = (levels.astype(jnp.bfloat16), (levels + HALF).astype(jnp.bfloat16))
    grad_copy.wait()
    hess_copy.wait()
    owners_copy.wait()
    route_ref[...] = route(owners[...] == feat_index, holders, earlier, plan.home_slots, route_ref.shape)
    for flat, tall in ((grad, grad_tall), (hess, hess_tall)):
        values = flat[...].astype(jnp.float32)
        for begin in range(0, row_count // LANES, 4):
            tiles = [jnp.broadcast_to(values[at : at + 1], (LANES, LANES)) for at in range(begin, begin + 4)]
            wide = jnp.concatenate(tiles, axis=1).astype(jnp.bfloat16)
            tall[begin * LANES : (begin + 4) * LANES, :] = wide.T
    zero = jnp.zeros((HALF, CHUNK), jnp.bfloat16)
    one = jnp.ones((HALF, CHUNK), jnp.bfloat16)

    def below(line, span):
        values = codes[line : line + 1, span].astype(jnp.float32)
        values = jnp.broadcast_to(values, (HALF, CHUNK)).astype(jnp.bfloat16)
        return [jnp.where(values <= level, one, zero) for level in level_parts]

    pltpu.make_async_copy(codes_hbm.at[pl.ds(0, 2 * count)], codes, code_sem).wait()
    for group in range(groups):
        total = None
        for begin in range(0, row_count, CHUNK):
            span = slice(begin, begin + CHUNK)
            first_rows, second_rows = [], []
            for pair in range(GROUP):
                line = 2 * (GROUP * group + pair)
                first_rows += below(line, span)
                second_rows += below(line + 1, span)
            first = jnp.concatenate(first_rows, axis=0)
            second = jnp.concatenate(second_rows, axis=0).T
            weighted = jnp.concatenate([second * grad_tall[span, :], second * hess_tall[span, :]], axis=1)
            product = jnp.dot(first, weighted, preferred_element_type=jnp.float32)
            total = product if total is None else total + product
        sums[group] = total
    lane = lax.broadcasted_iota(jnp.int32, (HALF, LANES), 1)
    for place in range(row_messages * per):
        message, at = place // per, place % per * HALF
        if place >= count:
            out_ref[message, at : at + HALF] = jnp.zeros((HALF, LANES), jnp.float32)
            continue
        group, pair = place // GROUP, place % GROUP
        block = None
        for quarter in range(4):
            top, left = pair * BINS + quarter // 2 * HALF, quarter % 2 * LANES
            piece = sums[group, top : top + HALF, left : left + LANES]
            moved = (quarter - pair) * BINS % LANES
            if moved:
                piece = pltpu.roll(piece, moved, 1)
            block = piece if block is None else jnp.where(lane >= quarter * BINS, piece, block)
        out_ref[message, at : at + HALF] = block


def cut_sums(plan, core, bin_codes, gradients, hessians, pair_list, owners):
    row_count = bin_codes.shape[1]
    start, count, per = plan.start[core], plan.count[core], plan.per[core]
    groups = count // GROUP
    tiles = row_count // LANES
    anywhere = pl.BlockSpec(memory_space=pl.ANY)
    in_vmem = pl.BlockSpec(memory_space=pltpu.VMEM)
    flat = (gradients.reshape(tiles, LANES), hessians.reshape(tiles, LANES), owners.reshape(1, plan.pair_count))
    operands = (pair_list.T, bin_codes) + flat
    return pl.pallas_call(
        functools.partial(cut_sums_kernel, plan, start, count, per),
        out_shape=(
            jax.ShapeDtypeStruct((plan.row_count, per * HALF, LANES), jnp.float32),
            jax.ShapeDtypeStruct((plan.home_slots + 8, CORES * plan.members * PARTS), jnp.float32),
        ),
        in_specs=[anywhere] * 5,
        out_specs=(in_vmem, in_vmem),
        scratch_shapes=[
            pltpu.SMEM((2, plan.pair_count), jnp.int32),
            pltpu.VMEM((2 * count, row_count), jnp.int32),
            pltpu.VMEM((tiles, LANES), jnp.bfloat16),
            pltpu.VMEM((tiles, LANES), jnp.bfloat16),
            pltpu.VMEM((1, plan.pair_count), jnp.int32),
            pltpu.VMEM((row_count, LANES), jnp.bfloat16),
            pltpu.VMEM((row_count, LANES), jnp.bfloat16),
            pltpu.VMEM((groups, GROUP * BINS, 2 * GROUP * BINS), jnp.float32),
            pltpu.SemaphoreType.DMA,
            pltpu.SemaphoreType.DMA((4,)),
        ],
        compiler_params=pltpu.CompilerParams(vmem_limit_bytes=SUMS_VMEM),
    )(*(pltpu.with_memory_space_constraint(operand, pltpu.HBM) for operand in operands))


def pair_gains(sums):
    upper = lax.broadcasted_iota(jnp.int32, sums.shape, 1) >= LANES // 2

    def margins(cum):
        end = jnp.where(upper, cum[:, 3 * BINS - 1 : 3 * BINS], cum[:, BINS - 1 : BINS])
        last = cum[HALF - 1 :]
        return cum, end, jnp.where(upper[:1], last, pltpu.roll(last, LANES // 2, 1)), last[:, 3 * BINS - 1 : 3 * BINS]

    grad_cum, grad_end, grad_col, grad_all = margins(sums)
    hess_cum, hess_end, hess_col, hess_all = margins(pltpu.roll(sums, LANES - BINS, 1))
    result = -(grad_all * grad_all) / (hess_all + LAMBDA_REG)
    for grad_part, hess_part in (
        (grad_cum, hess_cum),
        (grad_end - grad_cum, hess_end - hess_cum),
        (grad_col - grad_cum, hess_col - hess_cum),
        (grad_all - grad_end - grad_col + grad_cum, hess_all - hess_end - hess_col + hess_cum),
    ):
        result = result + grad_part * grad_part / (hess_part + LAMBDA_REG)
    return result


def gains_kernel(plan, start, count, per, parts_ref, out_ref, gains):
    share = BINS // plan.row_count
    lines = plan.row_count // 2
    total = parts_ref[0]
    for part in range(1, plan.row_count):
        total = total + parts_ref[part]
    place = per * seat(lax.axis_index("row"), plan.rows)
    first_pair = lax.axis_index("feat") // CORES * plan.chip_pairs + start + place
    line = lax.broadcasted_iota(jnp.int32, (1, LANES), 1)
    wide = lax.broadcasted_iota(jnp.int32, (lines, LANES), 1)
    best = jnp.zeros((1, LANES), jnp.float32)
    cuts = []
    for pair in range(per):
        result = pair_gains(total[pair * HALF : (pair + 1) * HALF])
        gains[pair] = result
        peak = jnp.max(result, axis=0, keepdims=True)
        top = jnp.max(jnp.where(line % (2 * BINS) < BINS, peak, -jnp.inf), axis=1, keepdims=True)
        best = jnp.where((line == first_pair + pair) & (place + pair < count), top, best)
        halves = []
        for half in range(2):
            laid = None
            for step in range(share):
                rows = gains[pair, pl.ds(step, lines, stride=share), :] if share > 1 else result
                moved = (step - 2 * half) * BINS % LANES
                if moved:
                    rows = pltpu.roll(rows, moved, 1)
                laid = rows if laid is None else jnp.where(wide >= step * BINS, rows, laid)
            halves.append(laid)
        cuts.append(halves)
    spot = lax.broadcasted_iota(jnp.int32, (PARTS, LANES), 0)
    messages = []
    for row in range(plan.row_count):
        message = jnp.broadcast_to(best, (PARTS, LANES))
        for pair in range(per):
            at = row % lines
            message = jnp.where(spot == pair, cuts[pair][row // lines][at : at + 1], message)
        messages.append(message)
    for place, member in enumerate(plan.order):
        out_ref[place] = messages[member // plan.chips]


def table_kernel(route_ref, near_ref, far_ref, table, best):
    ways = route_ref[...].astype(jnp.bfloat16)
    rest = jnp.concatenate([near_ref[...], far_ref[...]], axis=0)
    placed = jnp.zeros(route_ref.shape[:1] + rest.shape[1:], jnp.float32)
    for _ in range(3):
        part = rest.astype(jnp.bfloat16)
        rest = rest - part.astype(jnp.float32)
        placed = placed + jnp.dot(ways, part, preferred_element_type=jnp.float32)
    home_slots, width = table.shape
    table[...] = placed[:home_slots, :width]
    best[...] = placed[home_slots : home_slots + 1, : best.shape[1]]


def core_part(plan, core, *arguments):
    row_groups = [plan.rows]
    member_groups = [[member * CORES + side for member in plan.order] for side in range(CORES)]
    partial, ways = cut_sums(plan, core, *arguments)
    parts = lax.all_to_all(partial, "row", split_axis=0, concat_axis=0, tiled=True, axis_index_groups=row_groups)
    start, count, per = plan.start[core], plan.count[core], plan.per[core]
    in_vmem = pl.BlockSpec(memory_space=pltpu.VMEM)
    outgoing = pl.pallas_call(
        functools.partial(gains_kernel, plan, start, count, per),
        out_shape=jax.ShapeDtypeStruct((plan.members, PARTS, LANES), jnp.float32),
        in_specs=[in_vmem],
        out_specs=in_vmem,
        scratch_shapes=[pltpu.VMEM((per, HALF, LANES), jnp.float32)],
        compiler_params=pltpu.CompilerParams(vmem_limit_bytes=SMALL_VMEM),
    )(parts)
    near = lax.all_to_all(
        outgoing, ("row", "feat"), split_axis=0, concat_axis=0, tiled=True, axis_index_groups=member_groups
    )
    return near.reshape(plan.members * PARTS, LANES), ways


def shards(*arguments):
    feat_count = lax.axis_size("feat")
    plan = Plan(lax.axis_size("row"), feat_count, arguments[-1].shape[0])
    branches = [functools.partial(core_part, plan, core) for core in range(CORES)]
    near, ways = lax.cond(lax.axis_index("feat") % CORES == 0, *branches, *arguments)
    swap = [(feat, feat // CORES * CORES + (feat + 1) % CORES) for feat in range(feat_count)]
    far = lax.ppermute(near, "feat", swap)
    width = BINS // plan.row_count * BINS
    cut_table, best = pl.pallas_call(
        table_kernel,
        out_shape=(
            jax.ShapeDtypeStruct((plan.home_slots, width), jnp.float32),
            jax.ShapeDtypeStruct((1, plan.pair_count), jnp.float32),
        ),
        in_specs=[pl.BlockSpec(memory_space=pltpu.VMEM)] * 3,
        out_specs=[pl.BlockSpec(memory_space=pltpu.VMEM)] * 2,
        compiler_params=pltpu.CompilerParams(vmem_limit_bytes=SMALL_VMEM),
    )(ways, near, far)
    return (cut_table, best.reshape(plan.pair_count))


def solution(mesh):
    in_specs = (P(None, "row"), P("row"), P("row"), P(), P())
    out_specs = (P("feat", "row"), P())
    return jax.shard_map(shards, mesh=mesh, in_specs=in_specs, out_specs=out_specs, check_vma=False)
```

```python
import functools

import jax
import jax.numpy as jnp
from jax import lax
from jax.experimental import pallas as pl
from jax.experimental.pallas import tpu as pltpu
from jax.sharding import PartitionSpec as P

BINS = 32
LAMBDA_REG = 1.0
LANES = 128
CORES = 2
GROUP = 4
HALF = BINS // 2
PARTS = 4
CHUNK = 2048
HEAD = 5
LATE_HEAD = 5
ROW_ORDERS = {8: [5, 7, 0, 4, 3, 6, 1, 2]}
MEMBER_ORDERS = {16: [11, 10, 12, 5, 9, 0, 6, 3, 15, 8, 1, 14, 7, 2, 13, 4]}
SUMS_VMEM = 48 * 2**20
SMALL_VMEM = 4 * 2**20


class Plan:
    def __init__(self, row_count, feat_count, pair_count):
        self.row_count = row_count
        self.pair_count = pair_count
        self.chips = feat_count // CORES
        self.chip_pairs = pair_count // self.chips
        self.home_slots = 2 * pair_count // feat_count
        light = self.chip_pairs // GROUP // 4 * GROUP
        self.start = (0, light)
        self.count = (light, self.chip_pairs - light)
        self.per = tuple(-(-count // row_count) for count in self.count)
        self.rows = group_order(row_count, HEAD * row_count // 8, ROW_ORDERS)
        self.members = row_count * self.chips
        late_head = LATE_HEAD * row_count // 8 * self.chips + self.chips - 1
        self.order = group_order(self.members, late_head, MEMBER_ORDERS)


def group_order(size, head, orders):
    return orders.get(size, [head] + [member for member in range(size) if member != head])


def seat(member, order):
    head = order[0]
    if order[1:] == sorted(order[1:]):
        return jnp.where(member == head, 0, jnp.where(member < head, member + 1, member))
    place = jnp.zeros_like(member)
    for at, who in enumerate(order):
        place = jnp.where(member == who, at, place)
    return place


def sitter(place, order):
    head = order[0]
    if order[1:] == sorted(order[1:]):
        return jnp.where(place == 0, head, jnp.where(place <= head, place - 1, place))
    member = jnp.zeros_like(place)
    for at, who in enumerate(order):
        member = jnp.where(place == at, who, member)
    return member


def route_tables(plan):
    shape = (plan.pair_count, CORES * plan.members * PARTS)
    spot = lax.broadcasted_iota(jnp.int32, shape, 1)
    part, seated, other = spot % PARTS, spot // PARTS % plan.members, spot // (PARTS * plan.members)
    device = sitter(seated, plan.order)
    light = (lax.axis_index("feat") + other) % CORES == 0
    per, start, count = (jnp.where(light, values[0], values[1]) for values in (plan.per, plan.start, plan.count))
    place = seat(device // plan.chips, plan.rows) * per + part
    pair = device % plan.chips * plan.chip_pairs + start + place
    held = (part < per) & (place < count)
    holders = held & (pair == lax.broadcasted_iota(jnp.int32, shape, 0))
    square = (plan.pair_count, plan.pair_count)
    earlier = lax.broadcasted_iota(jnp.int32, square, 0) < lax.broadcasted_iota(jnp.int32, square, 1)
    return holders.astype(jnp.float32), earlier.astype(jnp.float32)


def route(mine, holders, earlier, home_slots, shape):
    owned = jnp.broadcast_to(mine.astype(jnp.float32), (8, mine.shape[1]))
    rank = jnp.dot(owned, earlier, preferred_element_type=jnp.float32)
    upper = lax.broadcasted_iota(jnp.int32, owned.shape, 0) == 0
    spread = jnp.dot(jnp.where(upper, owned, rank), holders, preferred_element_type=jnp.float32)
    slot = lax.broadcasted_iota(jnp.int32, shape, 0)
    taken = jnp.where(spread[1:2].astype(jnp.int32) == slot, spread[0:1], 0.0)
    best_row = jnp.where(lax.broadcasted_iota(jnp.int32, shape, 1) % PARTS == PARTS - 1, 1.0, 0.0)
    return jnp.where(slot < home_slots, taken, best_row)


def cut_sums_kernel(
    plan, start, count, per, pairs_hbm, codes_hbm, grad_hbm, hess_hbm, owners_hbm, out_ref, route_ref,
    pairs, codes, grad, hess, owners, grad_tall, hess_tall, sums, code_sem, small_sems,
):
    groups = count // GROUP
    row_count = codes.shape[1]
    row_messages = out_ref.shape[0]
    feat_index = lax.axis_index("feat")
    first_pair = feat_index // CORES * plan.chip_pairs + start
    pairs_copy = pltpu.make_async_copy(pairs_hbm, pairs, small_sems.at[0])
    grad_copy = pltpu.make_async_copy(grad_hbm, grad, small_sems.at[1])
    hess_copy = pltpu.make_async_copy(hess_hbm, hess, small_sems.at[2])
    owners_copy = pltpu.make_async_copy(owners_hbm, owners, small_sems.at[3])
    pairs_copy.start()
    grad_copy.start()
    hess_copy.start()
    owners_copy.start()
    holders, earlier = route_tables(plan)
    pairs_copy.wait()

    for line in range(2 * count):
        feature = pairs[line % 2, first_pair + line // 2]
        pltpu.make_async_copy(codes_hbm.at[pl.ds(feature, 1)], codes.at[pl.ds(line, 1)], code_sem).start()
    levels = lax.broadcasted_iota(jnp.int32, (HALF, 1), 0).astype(jnp.float32)
    level_parts = (levels.astype(jnp.bfloat16), (levels + HALF).astype(jnp.bfloat16))
    grad_copy.wait()
    hess_copy.wait()
    owners_copy.wait()
    route_ref[...] = route(owners[...] == feat_index, holders, earlier, plan.home_slots, route_ref.shape)
    for flat, tall in ((grad, grad_tall), (hess, hess_tall)):
        values = flat[...].astype(jnp.float32)
        for tile in range(row_count // LANES):
            square = jnp.broadcast_to(values[tile : tile + 1], (LANES, LANES)).astype(jnp.bfloat16)
            tall[tile * LANES : (tile + 1) * LANES, :] = square.T
    zero = jnp.zeros((HALF, CHUNK), jnp.bfloat16)
    one = jnp.ones((HALF, CHUNK), jnp.bfloat16)

    def below(line, span):
        values = codes[line : line + 1, span].astype(jnp.float32)
        values = jnp.broadcast_to(values, (HALF, CHUNK)).astype(jnp.bfloat16)
        return [jnp.where(values <= level, one, zero) for level in level_parts]

    pltpu.make_async_copy(codes_hbm.at[pl.ds(0, 2 * count)], codes, code_sem).wait()
    for group in range(groups):
        total = None
        for begin in range(0, row_count, CHUNK):
            span = slice(begin, begin + CHUNK)
            first_rows, second_rows = [], []
            for pair in range(GROUP):
                line = 2 * (GROUP * group + pair)
                first_rows += below(line, span)
                second_rows += below(line + 1, span)
            first = jnp.concatenate(first_rows, axis=0)
            second = jnp.concatenate(second_rows, axis=0).T
            weighted = jnp.concatenate([second * grad_tall[span, :], second * hess_tall[span, :]], axis=1)
            product = jnp.dot(first, weighted, preferred_element_type=jnp.float32)
            total = product if total is None else total + product
        sums[group] = total
    lane = lax.broadcasted_iota(jnp.int32, (HALF, LANES), 1)
    for place in range(row_messages * per):
        message, at = place // per, place % per * HALF
        if place >= count:
            out_ref[message, at : at + HALF] = jnp.zeros((HALF, LANES), jnp.float32)
            continue
        group, pair = place // GROUP, place % GROUP
        block = None
        for quarter in range(4):
            top, left = pair * BINS + quarter // 2 * HALF, quarter % 2 * LANES
            piece = sums[group, top : top + HALF, left : left + LANES]
            moved = (quarter - pair) * BINS % LANES
            if moved:
                piece = pltpu.roll(piece, moved, 1)
            block = piece if block is None else jnp.where(lane >= quarter * BINS, piece, block)
        out_ref[message, at : at + HALF] = block


def cut_sums(plan, core, bin_codes, gradients, hessians, pair_list, owners):
    row_count = bin_codes.shape[1]
    start, count, per = plan.start[core], plan.count[core], plan.per[core]
    groups = count // GROUP
    tiles = row_count // LANES
    anywhere = pl.BlockSpec(memory_space=pl.ANY)
    in_vmem = pl.BlockSpec(memory_space=pltpu.VMEM)
    flat = (gradients.reshape(tiles, LANES), hessians.reshape(tiles, LANES), owners.reshape(1, plan.pair_count))
    operands = (pair_list.T, bin_codes) + flat
    return pl.pallas_call(
        functools.partial(cut_sums_kernel, plan, start, count, per),
        out_shape=(
            jax.ShapeDtypeStruct((plan.row_count, per * HALF, LANES), jnp.float32),
            jax.ShapeDtypeStruct((plan.home_slots + 8, CORES * plan.members * PARTS), jnp.float32),
        ),
        in_specs=[anywhere] * 5,
        out_specs=(in_vmem, in_vmem),
        scratch_shapes=[
            pltpu.SMEM((2, plan.pair_count), jnp.int32),
            pltpu.VMEM((2 * count, row_count), jnp.int32),
            pltpu.VMEM((tiles, LANES), jnp.bfloat16),
            pltpu.VMEM((tiles, LANES), jnp.bfloat16),
            pltpu.VMEM((1, plan.pair_count), jnp.int32),
            pltpu.VMEM((row_count, LANES), jnp.bfloat16),
            pltpu.VMEM((row_count, LANES), jnp.bfloat16),
            pltpu.VMEM((groups, GROUP * BINS, 2 * GROUP * BINS), jnp.float32),
            pltpu.SemaphoreType.DMA,
            pltpu.SemaphoreType.DMA((4,)),
        ],
        compiler_params=pltpu.CompilerParams(vmem_limit_bytes=SUMS_VMEM),
    )(*(pltpu.with_memory_space_constraint(operand, pltpu.HBM) for operand in operands))


def pair_gains(sums):
    upper = lax.broadcasted_iota(jnp.int32, sums.shape, 1) >= LANES // 2

    def margins(cum):
        end = jnp.where(upper, cum[:, 3 * BINS - 1 : 3 * BINS], cum[:, BINS - 1 : BINS])
        last = cum[HALF - 1 :]
        return cum, end, jnp.where(upper[:1], last, pltpu.roll(last, LANES // 2, 1)), last[:, 3 * BINS - 1 : 3 * BINS]

    grad_cum, grad_end, grad_col, grad_all = margins(sums)
    hess_cum, hess_end, hess_col, hess_all = margins(pltpu.roll(sums, LANES - BINS, 1))
    result = -(grad_all * grad_all) / (hess_all + LAMBDA_REG)
    for grad_part, hess_part in (
        (grad_cum, hess_cum),
        (grad_end - grad_cum, hess_end - hess_cum),
        (grad_col - grad_cum, hess_col - hess_cum),
        (grad_all - grad_end - grad_col + grad_cum, hess_all - hess_end - hess_col + hess_cum),
    ):
        result = result + grad_part * grad_part / (hess_part + LAMBDA_REG)
    return result


def gains_kernel(plan, start, count, per, parts_ref, out_ref, gains):
    share = BINS // plan.row_count
    lines = plan.row_count // 2
    total = parts_ref[0]
    for part in range(1, plan.row_count):
        total = total + parts_ref[part]
    place = per * seat(lax.axis_index("row"), plan.rows)
    first_pair = lax.axis_index("feat") // CORES * plan.chip_pairs + start + place
    line = lax.broadcasted_iota(jnp.int32, (1, LANES), 1)
    wide = lax.broadcasted_iota(jnp.int32, (lines, LANES), 1)
    best = jnp.zeros((1, LANES), jnp.float32)
    cuts = []
    for pair in range(per):
        result = pair_gains(total[pair * HALF : (pair + 1) * HALF])
        gains[pair] = result
        peak = jnp.max(result, axis=0, keepdims=True)
        top = jnp.max(jnp.where(line % (2 * BINS) < BINS, peak, -jnp.inf), axis=1, keepdims=True)
        best = jnp.where((line == first_pair + pair) & (place + pair < count), top, best)
        halves = []
        for half in range(2):
            laid = None
            for step in range(share):
                rows = gains[pair, pl.ds(step, lines, stride=share), :] if share > 1 else result
                moved = (step - 2 * half) * BINS % LANES
                if moved:
                    rows = pltpu.roll(rows, moved, 1)
                laid = rows if laid is None else jnp.where(wide >= step * BINS, rows, laid)
            halves.append(laid)
        cuts.append(halves)
    spot = lax.broadcasted_iota(jnp.int32, (PARTS, LANES), 0)
    messages = []
    for row in range(plan.row_count):
        message = jnp.broadcast_to(best, (PARTS, LANES))
        for pair in range(per):
            at = row % lines
            message = jnp.where(spot == pair, cuts[pair][row // lines][at : at + 1], message)
        messages.append(message)
    for place, member in enumerate(plan.order):
        out_ref[place] = messages[member // plan.chips]


def table_kernel(route_ref, near_ref, far_ref, table, best):
    ways = route_ref[...].astype(jnp.bfloat16)
    rest = jnp.concatenate([near_ref[...], far_ref[...]], axis=0)
    placed = jnp.zeros(route_ref.shape[:1] + rest.shape[1:], jnp.float32)
    for _ in range(3):
        part = rest.astype(jnp.bfloat16)
        rest = rest - part.astype(jnp.float32)
        placed = placed + jnp.dot(ways, part, preferred_element_type=jnp.float32)
    home_slots, width = table.shape
    table[...] = placed[:home_slots, :width]
    best[...] = placed[home_slots : home_slots + 1, : best.shape[1]]


def core_part(plan, core, *arguments):
    row_groups = [plan.rows]
    member_groups = [[member * CORES + side for member in plan.order] for side in range(CORES)]
    partial, ways = cut_sums(plan, core, *arguments)
    parts = lax.all_to_all(partial, "row", split_axis=0, concat_axis=0, tiled=True, axis_index_groups=row_groups)
    start, count, per = plan.start[core], plan.count[core], plan.per[core]
    in_vmem = pl.BlockSpec(memory_space=pltpu.VMEM)
    outgoing = pl.pallas_call(
        functools.partial(gains_kernel, plan, start, count, per),
        out_shape=jax.ShapeDtypeStruct((plan.members, PARTS, LANES), jnp.float32),
        in_specs=[in_vmem],
        out_specs=in_vmem,
        scratch_shapes=[pltpu.VMEM((per, HALF, LANES), jnp.float32)],
        compiler_params=pltpu.CompilerParams(vmem_limit_bytes=SMALL_VMEM),
    )(parts)
    near = lax.all_to_all(
        outgoing, ("row", "feat"), split_axis=0, concat_axis=0, tiled=True, axis_index_groups=member_groups
    )
    return near.reshape(plan.members * PARTS, LANES), ways


def shards(*arguments):
    feat_count = lax.axis_size("feat")
    plan = Plan(lax.axis_size("row"), feat_count, arguments[-1].shape[0])
    branches = [functools.partial(core_part, plan, core) for core in range(CORES)]
    near, ways = lax.cond(lax.axis_index("feat") % CORES == 0, *branches, *arguments)
    swap = [(feat, feat // CORES * CORES + (feat + 1) % CORES) for feat in range(feat_count)]
    far = lax.ppermute(near, "feat", swap)
    width = BINS // plan.row_count * BINS
    cut_table, best = pl.pallas_call(
        table_kernel,
        out_shape=(
            jax.ShapeDtypeStruct((plan.home_slots, width), jnp.float32),
            jax.ShapeDtypeStruct((1, plan.pair_count), jnp.float32),
        ),
        in_specs=[pl.BlockSpec(memory_space=pltpu.VMEM)] * 3,
        out_specs=[pl.BlockSpec(memory_space=pltpu.VMEM)] * 2,
        compiler_params=pltpu.CompilerParams(vmem_limit_bytes=SMALL_VMEM),
    )(ways, near, far)
    return (cut_table, best.reshape(plan.pair_count))


def solution(mesh):
    in_specs = (P(None, "row"), P("row"), P("row"), P(), P())
    out_specs = (P("feat", "row"), P())
    return jax.shard_map(shards, mesh=mesh, in_specs=in_specs, out_specs=out_specs, check_vma=False)
```
